128 devices in a mesh: cuts: 16 (over y, x_hi, core), col: 8 (over z, x_lo).
Axes of the slice: x: 4 (x_hi: 2, x_lo: 2; x = x_hi * 2 + x_lo), y: 4, z: 4, core: 2. Of those that a mesh axis runs over, the one named last changes fastest.
Arguments:
- records: float32 [192, 512, 8192], P('cuts', None, 'col'), may hold values from -6 to 6
- row_lengths: int32 [192], P('cuts'), may hold values from 128 to 512, as said below
- row_mask: int32 [192, 512], P('cuts'), may hold values 0 or 1
- core_init: float32 [64, 64], replicated, may hold values from -6 to 6
- column_init: float32 [64, 8192], P(None, 'col'), may hold values from -6 to 6
- weight_init: float32 [192, 64], P('cuts'), may hold values from -6 to 6
Outputs:
- core_out: float32 [64, 64], replicated
- column_out: float32 [64, 8192], P(None, 'col')
- weight_out: float32 [192, 64], P('cuts')
The draws below stay inside these ranges and needn't reach their ends.
Inputs may be any that keep to these rules, and one draw needn't show every extreme that they name: Each slice uses its first row_lengths rows; some slice uses all 512.
All inputs are finite; a program needn't handle non-finite values. No bound on the sum of `row_mask` on one device may be relied on, other than what follows from the above.
Results may differ from the reference program's by a relative error of at most 0.0003.
Values sent between devices are 32-bit elements; how exact they have to be, the bound alone decides.
A program may use at most 128 MiB of HBM per device.

```python
import jax
import jax.numpy as jnp
from jax import lax

R = 64
J = 8192
PAD = 512
NS_STEPS = 8
SLICES = 192


def draw_row_lengths(key, part):
    lengths = jax.random.randint(key, (SLICES,), PAD // 4, PAD + 1)
    where = jax.random.randint(jax.random.fold_in(key, 7), (), 0, SLICES)
    return lengths.at[where].set(PAD).astype(jnp.int32)


def set_ends(values, key, least, top_value):
    longest = values.shape.index(max(values.shape))
    spots = []
    for shift in (0, 1):
        where = [jax.random.randint(jax.random.fold_in(key, axis), (), 0, length) for axis, length in enumerate(values.shape)]
        where[longest] = (where[longest] + shift) % values.shape[longest]
        spots.append(tuple(where))
    return values.at[spots[0]].set(least).at[spots[1]].set(top_value)


def block_levels(rng, shape, split, low, high):
    def one(axis_at, blocks):
        heights = jax.random.uniform(jax.random.fold_in(jax.random.fold_in(rng, 6), axis_at), (blocks,), jnp.float32, low / len(split), high / len(split))
        return jnp.repeat(jnp.exp(heights), shape[axis_at] // blocks).reshape((-1,) + (1,) * (len(shape) - axis_at - 1))

    factor_of = one(*split[0])
    for cut in split[1:]:
        factor_of = factor_of * one(*cut)
    return factor_of


def scatter_about(key, extent, spread, bound, shards=(), kind=jnp.bfloat16):
    gain = block_levels(key, extent, shards, -0.22, 0.18) if shards else 1.0
    drawn = jax.random.normal(key, extent, jnp.float32) * spread * gain
    return jnp.minimum(jnp.maximum(drawn, -bound), bound).astype(kind)


def setup_inputs(seed: int = 0) -> dict:
    splits = jax.random.split(jax.random.key(seed), 7)
    return {
        "records": scatter_about(splits[0], (SLICES, PAD, J), 1.0, 6.0, ((0, 16), (2, 8)), jnp.float32),
        "row_lengths": draw_row_lengths(jax.random.fold_in(splits[6], 71), 0),
        "row_mask": set_ends((jax.random.randint(splits[2], (SLICES, PAD), 0, 8) < 7).astype(jnp.int32), jax.random.fold_in(splits[2], 1), 0, 1),
        "core_init": scatter_about(splits[3], (R, R), 1.0, 6.0, (), jnp.float32),
        "column_init": scatter_about(splits[4], (R, J), 1.0, 6.0, ((1, 8),), jnp.float32),
        "weight_init": scatter_about(splits[5], (SLICES, R), 1.0, 6.0, ((0, 16),), jnp.float32),
    }


HP = lax.Precision.HIGHEST

def solve_sym(gram, rhs):
    lower = jnp.linalg.cholesky(gram)
    inner = lax.linalg.triangular_solve(lower, rhs, left_side=True, lower=True)
    return lax.linalg.triangular_solve(lower, inner, left_side=True, lower=True, transpose_a=True)

def reference(records, row_lengths, row_mask, core_init, column_init, weight_init):

    def one_slice(item):
        slab, length, maskrow, weight = item
        rows = lax.broadcasted_iota(jnp.int32, (PAD,), 0)
        valid = ((rows < length) & (maskrow == 1)).astype(jnp.float32)
        masked = slab * valid[:, None]
        proj = jnp.dot(column_init, masked.T, precision=HP)
        mixed = jnp.dot(core_init, weight[:, None] * proj, precision=HP)
        q = mixed / jnp.sqrt(jnp.sum(mixed * mixed) + 1e-06)
        for step in range(NS_STEPS):
            gram = jnp.dot(q, q.T, precision=HP)
            q = 1.5 * q - 0.5 * jnp.dot(gram, q, precision=HP)
        return jnp.dot(q, masked, precision=HP)
    projected = lax.map(one_slice, (records, row_lengths, row_mask, weight_init))
    slice_gram = jnp.dot(weight_init.T, weight_init, precision=HP)
    column_gram = jnp.dot(column_init, column_init.T, precision=HP)
    zterm = jnp.einsum('kaj,rj->kar', projected, column_init, precision=HP)
    h_terms = jnp.einsum('kar,kr->ar', zterm, weight_init, precision=HP)
    core = solve_sym(slice_gram * column_gram, h_terms.T).T
    core_n = core / jnp.sqrt(lax.optimization_barrier(jnp.sum(core * core, axis=0)) + 1e-06)[None, :]
    tproj = jnp.einsum('ar,kaj->krj', core_n, projected, precision=HP)
    v_terms = jnp.einsum('kr,krj->rj', weight_init, tproj, precision=HP)
    core_gram = jnp.dot(core_n.T, core_n, precision=HP)
    vt = solve_sym(slice_gram * core_gram, v_terms)
    v_gram = jnp.dot(vt, vt.T, precision=HP)
    norms = jnp.sqrt(jnp.diagonal(v_gram) + 1e-06)
    column_n = vt / norms[:, None]
    vn_gram = v_gram / (norms[:, None] * norms[None, :])
    w_terms = jnp.einsum('krj,rj->kr', tproj, column_n, precision=HP)
    weight_out = solve_sym(core_gram * vn_gram, w_terms.T).T
    return (core_n * jnp.sqrt(jnp.float32(R)), column_n * jnp.sqrt(jnp.float32(J)), weight_out)
```

```python
import functools

import jax
import jax.numpy as jnp
from jax import lax
from jax.experimental import pallas as pl
from jax.experimental.pallas import tpu as pltpu
from jax.sharding import PartitionSpec as P

R = 64
NS_STEPS = 8
CUTS = 16
COL = 8
SLICES = 12
SLOTS = 512
WIDTH = 1024
HALF = 256

F32 = jnp.float32
BF16 = jnp.bfloat16
HP = lax.Precision.HIGHEST
MESH = pl.DeviceIdType.MESH


def dot(a, b, ca=1, cb=0, precision=HP):
    return lax.dot_general(
        a, b, (((ca,), (cb,)), ((), ())), precision=precision, preferred_element_type=F32
    )


def fast(a, b, ca=1, cb=0):
    return dot(a, b, ca, cb, lax.Precision.DEFAULT)


def halves(x):
    high = x.astype(BF16)
    return high, (x - high.astype(F32)).astype(BF16)


def three(a, b_high, b_low, cb=0):
    a_high, a_low = halves(a)
    rows = a.shape[0]
    both = fast(jnp.concatenate([a_high, a_low], axis=0), b_high, 1, cb)
    return both[:rows] + both[rows:] + fast(a_high, b_low, 1, cb)


def iotas(shape):
    return lax.broadcasted_iota(jnp.int32, shape, 0), lax.broadcasted_iota(jnp.int32, shape, 1)


def diagonals(a):
    rows, cols = iotas(a.shape)
    kept = jnp.where(rows == cols, a, 0.0)
    return jnp.sum(kept, axis=0, keepdims=True), jnp.sum(kept, axis=1, keepdims=True)


def inverse(gram):
    rows, cols = iotas(gram.shape)
    d_row, d_col = diagonals(gram)
    s_row, s_col = lax.rsqrt(d_row), lax.rsqrt(d_col)

    def sweep(p, a):
        at_row, at_col = rows == p, cols == p
        row = jnp.sum(jnp.where(at_row, a, 0.0), axis=0, keepdims=True)
        col = jnp.sum(jnp.where(at_col, a, 0.0), axis=1, keepdims=True)
        pivot = jnp.sum(jnp.where(rows[:, :1] == p, col, 0.0), axis=0, keepdims=True)
        inv = 1.0 / pivot
        scaled = row * inv
        inner = a - col * scaled
        out = jnp.where(at_row, scaled, jnp.where(at_col, -col * inv, inner))
        return jnp.where(at_row & at_col, inv, out)

    return lax.fori_loop(0, R, sweep, gram * s_col * s_row) * s_col * s_row


def kernel(
    rec_ref, len_ref, mask_ref, core_ref, column_ref, weight_ref,
    core_out, column_out, weight_out,
    slab, vmask, psend, precv, pall, sgram, nall, yhi, ylo,
    sgbuf_y, sgbuf_q, cgbuf, hbuf_z, hbuf_y, hbuf_q, vsend, vrecv, vfull, fbuf, inv1,
    slab_sem, ps, pr, ss, sr, gs, gr, ns, nr, ws, wr, cs, cr, hs, hr, vs, vr, as_, ar, fs, fr,
):
    c = lax.axis_index("cuts")
    l = lax.axis_index("col")
    z, x = l // 2, l % 2
    y, q = c // 4, c % 4

    def col_to(src, dst, s, r, where):
        return pltpu.make_async_remote_copy(
            src_ref=src, dst_ref=dst, send_sem=s, recv_sem=r,
            device_id={"col": where}, device_id_type=MESH,
        )

    def cuts_to(src, dst, s, r, where):
        return pltpu.make_async_remote_copy(
            src_ref=src, dst_ref=dst, send_sem=s, recv_sem=r,
            device_id={"cuts": where}, device_id_type=MESH,
        )

    def col_at(d):
        return lax.rem(l + d, COL)

    def cuts_at(d):
        return lax.rem(c + d, CUTS)

    def z_at(d):
        return lax.rem(z + d, 4) * 2 + x

    def y_at(d):
        return lax.rem(y + d, 4) * 4 + q

    def q_at(d):
        return y * 4 + lax.rem(q + d, 4)

    def slab_copy(k):
        return pltpu.make_async_copy(rec_ref.at[k], slab.at[k], slab_sem.at[k])

    def slice_of(t):
        return lax.rem(z + 2 + t // 3, 4) * 3 + t % 3

    def start_slab(t, carry):
        slab_copy(slice_of(t)).start()
        return carry

    lax.fori_loop(0, SLICES, start_slab, 0)

    barrier = pltpu.get_barrier_semaphore()
    for d in range(1, COL):
        pl.semaphore_signal(barrier, inc=1, device_id={"col": col_at(d)}, device_id_type=MESH)
    for d in range(1, CUTS):
        pl.semaphore_signal(barrier, inc=1, device_id={"cuts": cuts_at(d)}, device_id_type=MESH)

    slot = lax.broadcasted_iota(jnp.int32, (SLICES, SLOTS), 1)
    vmask[...] = jnp.where((slot < len_ref[...]) & (mask_ref[...] == 1), 1.0, 0.0)
    weight = weight_ref[...]
    column = column_ref[...]
    c_high, c_low = halves(column)
    cgbuf[l] = dot(column, column, 1, 1)
    sgbuf_y[y] = dot(weight, weight, 0, 0)

    pl.semaphore_wait(barrier, COL + CUTS - 2)

    for d in range(1, COL):
        to = col_at(d)
        col_to(cgbuf.at[l], cgbuf.at[l], cs.at[to], cr.at[l], to).start()
    for d in range(1, 4):
        to = lax.rem(y + d, 4)
        cuts_to(sgbuf_y.at[y], sgbuf_y.at[y], ws.at[0, to], wr.at[0, y], y_at(d)).start()

    c_both = jnp.concatenate([c_high, c_low], axis=0)

    def project(t, carry):
        k = slice_of(t)
        j = lax.rem(k, 3)
        slab_copy(k).wait()
        for h in range(2):
            owner = (k // 3) * 2 + h
            high, low = halves(slab[k, h * HALF:(h + 1) * HALF, :])
            both = fast(c_both, high, 1, 1)
            part = both[:R] + both[R:] + fast(c_high, low, 1, 1)

            @pl.when(owner == l)
            def keep():
                precv[l, j] = part

            @pl.when(owner != l)
            def send():
                psend[owner, j] = part
                col_to(psend.at[owner, j], precv.at[l, j], ps.at[owner, j], pr.at[l, j], owner).start()
        return carry

    lax.fori_loop(0, SLICES, project, 0)

    for d in range(1, 4):
        frm = lax.rem(y + d, 4)
        cuts_to(sgbuf_y.at[frm], sgbuf_y.at[frm], ws.at[0, frm], wr.at[0, frm], y_at(d)).wait_recv()
    sgbuf_q[q] = sgbuf_y[0] + sgbuf_y[1] + sgbuf_y[2] + sgbuf_y[3]
    for d in range(1, 4):
        to = lax.rem(q + d, 4)
        cuts_to(sgbuf_q.at[q], sgbuf_q.at[q], ws.at[1, to], wr.at[1, q], q_at(d)).start()
    for d in range(1, COL):
        frm = col_at(d)
        col_to(cgbuf.at[frm], cgbuf.at[frm], cs.at[frm], cr.at[frm], frm).wait_recv()
    column_gram = cgbuf[0]
    for i in range(1, COL):
        column_gram = column_gram + cgbuf[i]
    for d in range(1, 4):
        frm = lax.rem(q + d, 4)
        cuts_to(sgbuf_q.at[frm], sgbuf_q.at[frm], ws.at[1, frm], wr.at[1, frm], q_at(d)).wait_recv()
    slice_gram = sgbuf_q[0] + sgbuf_q[1] + sgbuf_q[2] + sgbuf_q[3]
    inv1[...] = inverse(slice_gram * column_gram)

    def reduce(j, carry):
        for d in range(1, COL):
            frm = col_at(d)
            col_to(psend.at[frm, j], precv.at[frm, j], ps.at[frm, j], pr.at[frm, j], frm).wait_recv()
        total = precv[0, j]
        for i in range(1, COL):
            total = total + precv[i, j]
        mask = vmask[pl.ds(z * 3 + j, 1), pl.ds(pl.multiple_of(x * HALF, HALF), HALF)]
        total = total * mask
        pall[l, j] = total
        sgram[x, j] = dot(total, total, 1, 1)
        return carry

    lax.fori_loop(0, 3, reduce, 0)

    other = z * 2 + (1 - x)
    gram_copy = col_to(sgram.at[x], sgram.at[x], ss, sr.at[x], other)
    gram_copy.start()
    for d in range(1, COL):
        to = col_at(d)
        col_to(pall.at[l], pall.at[l], gs.at[to], gr.at[l], to).start()
    col_to(sgram.at[1 - x], sgram.at[1 - x], ss, sr.at[1 - x], other).wait_recv()

    rows, cols = iotas((R, R))
    eye = jnp.where(rows == cols, 1.0, 0.0)
    grams, mixes, scales, sums, wrows = [], [], [], [], []
    for j in range(3):
        wrow = weight_ref[pl.ds(z * 3 + j, 1), :]
        s = sgram[0, j] + sgram[1, j]
        mix = core_ref[...] * wrow
        g = dot(dot(mix, s), mix, 1, 1)
        trace = jnp.sum(jnp.where(rows == cols, g, 0.0), axis=(0, 1), keepdims=True) + 1e-06
        grams.append(g / trace)
        mixes.append(mix)
        scales.append(lax.rsqrt(trace))
        sums.append(s)
        wrows.append(wrow)

    def newton(_, carry):
        gs_, ps_ = carry
        next_g, next_p = [], []
        for g, p in zip(gs_, ps_):
            square = dot(g, g)
            next_p.append(1.5 * p - 0.5 * dot(g, p))
            next_g.append(2.25 * g - 1.5 * square + 0.25 * dot(square, g))
        return next_g, next_p

    grams, polys = lax.fori_loop(0, NS_STEPS - 1, newton, (grams, [eye] * 3))
    h_sum = jnp.zeros((R, R), F32)
    for j in range(3):
        poly = 1.5 * polys[j] - 0.5 * dot(grams[j], polys[j])
        turned = dot(mixes[j], poly, 0, 0) * scales[j]
        nall[z, j * R:(j + 1) * R, :] = turned
        h_sum = h_sum + dot(turned, sums[j], 0, 0) * wrows[j]
    hbuf_z[z] = h_sum
    for d in range(1, 4):
        to = lax.rem(z + d, 4)
        col_to(hbuf_z.at[z], hbuf_z.at[z], hs.at[0, to], hr.at[0, z], z_at(d)).start()
    for d in range(1, 4):
        to = lax.rem(z + d, 4)
        col_to(nall.at[z], nall.at[z], ns.at[to], nr.at[z], z_at(d)).start()

    for d in range(1, COL):
        frm = col_at(d)
        col_to(pall.at[frm], pall.at[frm], gs.at[frm], gr.at[frm], frm).wait_recv()

    def second(k, carry):
        zz, j = k // 3, lax.rem(k, 3)
        acc = jnp.zeros((R, WIDTH), F32)
        for h in range(2):
            high, low = halves(slab[k, h * HALF:(h + 1) * HALF, :])
            acc = acc + three(pall[zz * 2 + h, j], high, low)
        high, low = halves(acc)
        at = pl.ds(pl.multiple_of(k * R, R), R)
        yhi[at, :] = high
        ylo[at, :] = low
        return carry

    lax.fori_loop(0, 4, second, 0)
    for d in range(1, 4):
        frm = lax.rem(z + d, 4)
        col_to(hbuf_z.at[frm], hbuf_z.at[frm], hs.at[0, frm], hr.at[0, frm], z_at(d)).wait_recv()
    hbuf_y[y] = hbuf_z[0] + hbuf_z[1] + hbuf_z[2] + hbuf_z[3]
    for d in range(1, 4):
        to = lax.rem(y + d, 4)
        cuts_to(hbuf_y.at[y], hbuf_y.at[y], hs.at[1, to], hr.at[1, y], y_at(d)).start()
    lax.fori_loop(4, 8, second, 0)
    for d in range(1, 4):
        frm = lax.rem(y + d, 4)
        cuts_to(hbuf_y.at[frm], hbuf_y.at[frm], hs.at[1, frm], hr.at[1, frm], y_at(d)).wait_recv()
    hbuf_q[q] = hbuf_y[0] + hbuf_y[1] + hbuf_y[2] + hbuf_y[3]
    for d in range(1, 4):
        to = lax.rem(q + d, 4)
        cuts_to(hbuf_q.at[q], hbuf_q.at[q], hs.at[2, to], hr.at[2, q], q_at(d)).start()
    lax.fori_loop(8, SLICES, second, 0)
    for d in range(1, 4):
        frm = lax.rem(z + d, 4)
        col_to(nall.at[frm], nall.at[frm], ns.at[frm], nr.at[frm], z_at(d)).wait_recv()
    for d in range(1, 4):
        frm = lax.rem(q + d, 4)
        cuts_to(hbuf_q.at[frm], hbuf_q.at[frm], hs.at[2, frm], hr.at[2, frm], q_at(d)).wait_recv()
    h_terms = hbuf_q[0] + hbuf_q[1] + hbuf_q[2] + hbuf_q[3]

    core_t = dot(inv1[...], h_terms, 1, 1)
    core_t = core_t * lax.rsqrt(jnp.sum(core_t * core_t, axis=1, keepdims=True) + 1e-06)
    core_gram = dot(core_t, core_t, 1, 1)
    stacked = nall[...].reshape(SLICES * R, R)
    mixed = dot(core_t, stacked, 1, 1)
    k_of, s_of = iotas((SLICES, SLICES * R))
    spread = jnp.where(s_of // R == k_of, 1.0, 0.0)
    weighted = mixed * dot(weight, spread, 0, 0)
    v_local = three(weighted, yhi[...], ylo[...])
    for i in range(CUTS):
        part = v_local[(i // 8) * 32:(i // 8) * 32 + 32, (i % 8) * 128:(i % 8) * 128 + 128]
        vsend[i] = part
    vrecv[c] = vsend[c]
    for d in range(1, CUTS):
        to = cuts_at(d)
        cuts_to(vsend.at[to], vrecv.at[c], vs.at[to], vr.at[c], to).start()
    core_out[...] = dot(eye, core_t, 1, 1) * 8.0
    inv2 = inverse(slice_gram * core_gram)
    for d in range(1, CUTS):
        frm = cuts_at(d)
        cuts_to(vsend.at[frm], vrecv.at[frm], vs.at[frm], vr.at[frm], frm).wait_recv()
    total = vrecv[0]
    for i in range(1, CUTS):
        total = total + vrecv[i]
    vfull[c] = total
    for d in range(1, CUTS):
        to = cuts_at(d)
        cuts_to(vfull.at[c], vfull.at[c], as_.at[to], ar.at[c], to).start()
    for d in range(1, CUTS):
        frm = cuts_at(d)
        cuts_to(vfull.at[frm], vfull.at[frm], as_.at[frm], ar.at[frm], frm).wait_recv()
    v_terms = jnp.concatenate(
        [jnp.concatenate([vfull[i * 8 + b] for b in range(8)], axis=1) for i in range(2)], axis=0
    )
    vt = dot(inv2, v_terms)
    fbuf[l, :R, :] = dot(vt, vt, 1, 1)
    found = mixed * three(vt, yhi[...], ylo[...], 1)
    fbuf[l, R:R + SLICES, :] = dot(spread, found, 1, 1)
    for d in range(1, COL):
        to = col_at(d)
        col_to(fbuf.at[l], fbuf.at[l], fs.at[to], fr.at[l], to).start()
    for d in range(1, COL):
        frm = col_at(d)
        col_to(fbuf.at[frm], fbuf.at[frm], fs.at[frm], fr.at[frm], frm).wait_recv()
    total = fbuf[0]
    for i in range(1, COL):
        total = total + fbuf[i]
    v_gram = total[:R]
    w_terms = total[R:R + SLICES]
    d_row, d_col = diagonals(v_gram)
    n_row, n_col = lax.rsqrt(d_row + 1e-06), lax.rsqrt(d_col + 1e-06)
    column_out[...] = vt * (n_col * (8192.0 ** 0.5))
    inv3 = inverse(core_gram * (v_gram * n_col * n_row))
    weight_out[...] = dot(w_terms * n_row, inv3)

    for d in range(1, COL):
        to = col_at(d)
        col_to(cgbuf.at[l], cgbuf.at[l], cs.at[to], cr.at[l], to).wait_send()
        col_to(pall.at[l], pall.at[l], gs.at[to], gr.at[l], to).wait_send()
        col_to(fbuf.at[l], fbuf.at[l], fs.at[to], fr.at[l], to).wait_send()
        for j in range(3):
            col_to(psend.at[to, j], precv.at[l, j], ps.at[to, j], pr.at[l, j], to).wait_send()
    gram_copy.wait_send()
    for d in range(1, 4):
        to = lax.rem(z + d, 4)
        col_to(hbuf_z.at[z], hbuf_z.at[z], hs.at[0, to], hr.at[0, z], z_at(d)).wait_send()
        col_to(nall.at[z], nall.at[z], ns.at[to], nr.at[z], z_at(d)).wait_send()
        to = lax.rem(y + d, 4)
        cuts_to(sgbuf_y.at[y], sgbuf_y.at[y], ws.at[0, to], wr.at[0, y], y_at(d)).wait_send()
        cuts_to(hbuf_y.at[y], hbuf_y.at[y], hs.at[1, to], hr.at[1, y], y_at(d)).wait_send()
        to = lax.rem(q + d, 4)
        cuts_to(sgbuf_q.at[q], sgbuf_q.at[q], ws.at[1, to], wr.at[1, q], q_at(d)).wait_send()
        cuts_to(hbuf_q.at[q], hbuf_q.at[q], hs.at[2, to], hr.at[2, q], q_at(d)).wait_send()
    for d in range(1, CUTS):
        to = cuts_at(d)
        cuts_to(vsend.at[to], vrecv.at[c], vs.at[to], vr.at[c], to).wait_send()
        cuts_to(vfull.at[c], vfull.at[c], as_.at[to], ar.at[c], to).wait_send()


def shards(records, row_lengths, row_mask, core_init, column_init, weight_init):
    vmem = pl.BlockSpec(memory_space=pltpu.VMEM)
    dma = pltpu.SemaphoreType.DMA
    return pl.pallas_call(
        kernel,
        out_shape=(
            jax.ShapeDtypeStruct((R, R), F32),
            jax.ShapeDtypeStruct((R, WIDTH), F32),
            jax.ShapeDtypeStruct((SLICES, R), F32),
        ),
        in_specs=[pl.BlockSpec(memory_space=pl.ANY)] + [vmem] * 5,
        out_specs=(vmem,) * 3,
        scratch_shapes=[
            pltpu.VMEM((SLICES, SLOTS, WIDTH), F32),
            pltpu.VMEM((SLICES, SLOTS), F32),
            pltpu.VMEM((COL, 3, R, HALF), F32),
            pltpu.VMEM((COL, 3, R, HALF), F32),
            pltpu.VMEM((COL, 3, R, HALF), F32),
            pltpu.VMEM((2, 3, R, R), F32),
            pltpu.VMEM((4, 3 * R, R), F32),
            pltpu.VMEM((SLICES * R, WIDTH), BF16),
            pltpu.VMEM((SLICES * R, WIDTH), BF16),
            pltpu.VMEM((4, R, R), F32),
            pltpu.VMEM((4, R, R), F32),
            pltpu.VMEM((COL, R, R), F32),
            pltpu.VMEM((4, R, R), F32),
            pltpu.VMEM((4, R, R), F32),
            pltpu.VMEM((4, R, R), F32),
            pltpu.VMEM((CUTS, 32, 128), F32),
            pltpu.VMEM((CUTS, 32, 128), F32),
            pltpu.VMEM((CUTS, 32, 128), F32),
            pltpu.VMEM((COL, 80, R), F32),
            pltpu.VMEM((R, R), F32),
            dma((SLICES,)),
            dma((COL, 3)), dma((COL, 3)),
            dma, dma((2,)),
            dma((COL,)), dma((COL,)),
            dma((4,)), dma((4,)),
            dma((2, 4)), dma((2, 4)),
            dma((COL,)), dma((COL,)),
            dma((3, 4)), dma((3, 4)),
            dma((CUTS,)), dma((CUTS,)),
            dma((CUTS,)), dma((CUTS,)),
            dma((COL,)), dma((COL,)),
        ],
        compiler_params=pltpu.CompilerParams(
            collective_id=0, has_side_effects=True, vmem_limit_bytes=60 * 1024 * 1024
        ),
    )(records, row_lengths[:, None], row_mask, core_init, column_init, weight_init)


def solution(mesh):
    in_specs = (
        P("cuts", None, "col"),
        P("cuts"),
        P("cuts", None),
        P(),
        P(None, "col"),
        P("cuts", None),
    )
    out_specs = (P(), P(None, "col"), P("cuts", None))
    return jax.shard_map(shards, mesh=mesh, in_specs=in_specs, out_specs=out_specs, check_vma=False)
```

```python
import functools

import jax
import jax.numpy as jnp
from jax import lax
from jax.experimental import pallas as pl
from jax.experimental.pallas import tpu as pltpu
from jax.sharding import PartitionSpec as P

R = 64
NS_STEPS = 8
CUTS = 16
COL = 8
SLICES = 12
SLOTS = 512
WIDTH = 1024
HALF = 256

F32 = jnp.float32
BF16 = jnp.bfloat16
HP = lax.Precision.HIGHEST
MESH = pl.DeviceIdType.MESH


def dot(a, b, ca=1, cb=0, precision=HP):
    return lax.dot_general(
        a, b, (((ca,), (cb,)), ((), ())), precision=precision, preferred_element_type=F32
    )


def fast(a, b, ca=1, cb=0):
    return dot(a, b, ca, cb, lax.Precision.DEFAULT)


def halves(x):
    high = x.astype(BF16)
    return high, (x - high.astype(F32)).astype(BF16)


def three(a, b_high, b_low, cb=0):
    a_high, a_low = halves(a)
    rows = a.shape[0]
    both = fast(jnp.concatenate([a_high, a_low], axis=0), b_high, 1, cb)
    return both[:rows] + both[rows:] + fast(a_high, b_low, 1, cb)


def iotas(shape):
    return lax.broadcasted_iota(jnp.int32, shape, 0), lax.broadcasted_iota(jnp.int32, shape, 1)


def diagonals(a):
    rows, cols = iotas(a.shape)
    kept = jnp.where(rows == cols, a, 0.0)
    return jnp.sum(kept, axis=0, keepdims=True), jnp.sum(kept, axis=1, keepdims=True)


def inverse(gram):
    rows, cols = iotas(gram.shape)
    d_row, d_col = diagonals(gram)
    s_row, s_col = lax.rsqrt(d_row), lax.rsqrt(d_col)

    def sweep(p, a):
        at_row, at_col = rows == p, cols == p
        row = jnp.sum(jnp.where(at_row, a, 0.0), axis=0, keepdims=True)
        col = jnp.sum(jnp.where(at_col, a, 0.0), axis=1, keepdims=True)
        pivot = jnp.sum(jnp.where(rows[:, :1] == p, col, 0.0), axis=0, keepdims=True)
        inv = 1.0 / pivot
        scaled = row * inv
        inner = a - col * scaled
        out = jnp.where(at_row, scaled, jnp.where(at_col, -col * inv, inner))
        return jnp.where(at_row & at_col, inv, out)

    return lax.fori_loop(0, R, sweep, gram * s_col * s_row) * s_col * s_row


def kernel(
    len_ref, rec_ref, mask_ref, core_ref, column_ref, weight_ref,
    total_out, vt_out, core_out, gram_out,
    slab, vmask, keep, xsend, xrecv, zsend, zrecv, z0send, z0recv, x0send, x0recv, pall0, pall12,
    sgram, nall, yhi, ylo,
    sgbuf_y, sgbuf_q, cgbuf_z, cgbuf_x, hbuf_y, hbuf_z, hbuf_q, vsend, vrecv, vfull, fbuf, inv1,
    slab_sem, xs, xr, zs, zr, z0s, z0r, x0s, x0r, ss, sr, gxs, gxr, gzs, gzr, g0s, g0r,
    ns, nr, ws, wr, cs, cr, hs, hr, vs, vr, as_, ar, fs, fr,
):
    c = lax.axis_index("cuts")
    l = lax.axis_index("col")
    z, x = l // 2, l % 2
    y, q = c // 4, c % 4
    other = z * 2 + (1 - x)

    sent = []

    def send(copy):
        copy.start()
        sent.append(copy)

    def col_to(src, dst, s, r, where):
        return pltpu.make_async_remote_copy(
            src_ref=src, dst_ref=dst, send_sem=s, recv_sem=r,
            device_id={"col": where}, device_id_type=MESH,
        )

    def cuts_to(src, dst, s, r, where):
        return pltpu.make_async_remote_copy(
            src_ref=src, dst_ref=dst, send_sem=s, recv_sem=r,
            device_id={"cuts": where}, device_id_type=MESH,
        )

    def col_at(d):
        return lax.rem(l + d, COL)

    def cuts_at(d):
        return lax.rem(c + d, CUTS)

    def z_plus(d):
        return lax.rem(z + d, 4)

    def exchange(buf, s, r, here, axis, stage):
        for d in (2, 1, 3):
            there = lax.rem(here + d, 4)
            if axis == "z":
                go, to = col_to, there * 2 + x
            else:
                go, to = cuts_to, (there * 4 + q if axis == "y" else y * 4 + there)
            if stage == "send":
                send(go(buf.at[here], buf.at[here], s.at[there], r.at[here], to))
            else:
                go(buf.at[there], buf.at[there], s.at[there], r.at[there], to).wait_recv()

    def sum4(buf):
        return (buf[0] + buf[1]) + (buf[2] + buf[3])

    def slab_copy(k):
        return pltpu.make_async_copy(rec_ref.at[k], slab.at[k], slab_sem.at[k])

    far = (2, 1, 3, 0)
    for d in far:
        for j in (1, 2):
            slab_copy(z_plus(d) * 3 + j).start()
    for d in far:
        slab_copy(z_plus(d) * 3).start()

    barrier = pltpu.get_barrier_semaphore()
    pl.semaphore_signal(barrier, inc=1, device_id={"col": other}, device_id_type=MESH)
    for d in range(1, 4):
        for axis, to in (
            ("col", z_plus(d) * 2 + x),
            ("cuts", lax.rem(y + d, 4) * 4 + q),
            ("cuts", y * 4 + lax.rem(q + d, 4)),
        ):
            pl.semaphore_signal(barrier, inc=1, device_id={axis: to}, device_id_type=MESH)

    slot = lax.broadcasted_iota(jnp.int32, (1, SLOTS), 1)
    for k in range(SLICES):
        vmask[k:k + 1, :] = jnp.where((slot < len_ref[k]) & (mask_ref[k:k + 1, :] == 1), 1.0, 0.0)
    weight = weight_ref[...]
    column = column_ref[...]
    c_high, c_low = halves(column)
    c_both = jnp.concatenate([c_high, c_low], axis=0)
    cgbuf_z[z] = dot(column, column, 1, 1)
    sgbuf_y[y] = dot(weight, weight, 0, 0)

    def part_of(k, h):
        high, low = halves(slab[k, pl.ds(pl.multiple_of(h * HALF, HALF), HALF), :])
        both = fast(c_both, high, 1, 1)
        return both[:R] + both[R:] + fast(c_high, low, 1, 1)

    def pair(zz):
        def one(j, carry):
            k = zz * 3 + 1 + j
            slab_copy(k).wait()
            xsend[zz, j] = part_of(k, 1 - x)
            keep[zz, j] = part_of(k, x)
            return carry

        lax.fori_loop(0, 2, one, 0)

    def pair_send(zz):
        send(col_to(xsend.at[zz], xrecv.at[zz], xs.at[zz], xr.at[zz], other))

    def pair_sum(zz):
        col_to(xsend.at[zz], xrecv.at[zz], xs.at[zz], xr.at[zz], other).wait_recv()
        zsend[zz] = keep[zz] + xrecv[zz]

    def pair_pass(zz):
        pair_sum(zz)
        send(col_to(zsend.at[zz], zrecv.at[z], zs.at[zz], zr.at[z], zz * 2 + x))

    def single(zz):
        slab_copy(zz * 3).wait()

        def one(h, carry):
            z0send[zz, h] = part_of(zz * 3, h)
            return carry

        lax.fori_loop(0, 2, one, 0)

    def single_send(zz):
        send(col_to(z0send.at[zz], z0recv.at[z], z0s.at[zz], z0r.at[z], zz * 2 + x))

    pair(z_plus(2))
    pl.semaphore_wait(barrier, 10)
    pair_send(z_plus(2))
    exchange(sgbuf_y, ws.at[0], wr.at[0], y, "y", "send")
    exchange(cgbuf_z, cs, cr, z, "z", "send")
    pair(z_plus(1))
    pair_send(z_plus(1))
    pair(z_plus(3))
    pair_send(z_plus(3))
    pair_pass(z_plus(2))
    exchange(sgbuf_y, ws.at[0], wr.at[0], y, "y", "wait")
    sgbuf_q[q] = sum4(sgbuf_y)
    exchange(sgbuf_q, ws.at[1], wr.at[1], q, "q", "send")
    exchange(cgbuf_z, cs, cr, z, "z", "wait")
    cgbuf_x[x] = sum4(cgbuf_z)
    send(col_to(cgbuf_x.at[x], cgbuf_x.at[x], cs.at[4], cr.at[4], other))
    pair(z)
    pair_send(z)
    pair_pass(z_plus(1))
    single(z_plus(2))
    single_send(z_plus(2))
    pair_pass(z_plus(3))
    single(z_plus(1))
    single_send(z_plus(1))
    single(z_plus(3))
    single_send(z_plus(3))
    single(z)
    pair_sum(z)
    for d in far[:3]:
        zz = z_plus(d)
        col_to(z0send.at[zz], z0recv.at[zz], z0s.at[zz], z0r.at[zz], zz * 2 + x).wait_recv()
    x0send[...] = (z0send[z] + z0recv[z_plus(1)]) + (z0recv[z_plus(2)] + z0recv[z_plus(3)])
    send(col_to(x0send, x0recv, x0s, x0r, other))

    def mask_of(j, h):
        return vmask[pl.ds(z * 3 + j, 1), pl.ds(pl.multiple_of(h * HALF, HALF), HALF)]

    for d in far[:3]:
        zz = z_plus(d)
        col_to(zsend.at[zz], zrecv.at[zz], zs.at[zz], zr.at[zz], zz * 2 + x).wait_recv()
    for j in range(2):
        total = (zsend[z, j] + zrecv[z_plus(1), j]) + (zrecv[z_plus(2), j] + zrecv[z_plus(3), j])
        total = total * mask_of(1 + j, x)
        pall12[z, x, j] = total
        sgram[x, j] = dot(total, total, 1, 1)
    send(col_to(sgram.at[x], sgram.at[x], ss, sr.at[x], other))
    send(col_to(pall12.at[z, x], pall12.at[z, x], gxs.at[z], gxr.at[z], other))
    for d in far[:3]:
        zz = z_plus(d)
        send(col_to(pall12.at[z, x], pall12.at[z, x], gzs.at[zz], gzr.at[z], zz * 2 + x))

    exchange(sgbuf_q, ws.at[1], wr.at[1], q, "q", "wait")
    slice_gram = sum4(sgbuf_q)
    col_to(cgbuf_x.at[1 - x], cgbuf_x.at[1 - x], cs.at[4], cr.at[4], other).wait_recv()
    inv1[...] = inverse(slice_gram * (cgbuf_x[0] + cgbuf_x[1]))

    col_to(x0send, x0recv, x0s, x0r, other).wait_recv()
    gram0 = jnp.zeros((R, R), F32)
    for h in range(2):
        total = (x0send[h] + x0recv[h]) * mask_of(0, h)
        pall0[z, h] = total
        gram0 = gram0 + dot(total, total, 1, 1)
    for d in far[:3]:
        zz = z_plus(d)
        send(col_to(pall0.at[z], pall0.at[z], g0s.at[zz], g0r.at[z], zz * 2 + x))
    col_to(sgram.at[1 - x], sgram.at[1 - x], ss, sr.at[1 - x], other).wait_recv()

    rows, cols = iotas((R, R))
    eye = jnp.where(rows == cols, 1.0, 0.0)
    sums = [gram0, sgram[0, 0] + sgram[1, 0], sgram[0, 1] + sgram[1, 1]]
    grams, mixes, scales, wrows = [], [], [], []
    for j in range(3):
        wrow = weight_ref[pl.ds(z * 3 + j, 1), :]
        mix = core_ref[...] * wrow
        g = dot(dot(mix, sums[j]), mix, 1, 1)
        trace = jnp.sum(jnp.where(rows == cols, g, 0.0), axis=(0, 1), keepdims=True) + 1e-06
        grams.append(g / trace)
        mixes.append(mix)
        scales.append(lax.rsqrt(trace))
        wrows.append(wrow)

    def newton(_, carry):
        gs_, ps_ = carry
        next_g, next_p = [], []
        for g, p in zip(gs_, ps_):
            square = dot(g, g)
            next_p.append(1.5 * p - 0.5 * dot(g, p))
            next_g.append(2.25 * g - 1.5 * square + 0.25 * dot(square, g))
        return next_g, next_p

    def forward(d):
        zz = z_plus(d)
        col_to(pall12.at[zz, x], pall12.at[zz, x], gzs.at[zz], gzr.at[zz], zz * 2 + x).wait_recv()
        send(col_to(pall12.at[zz, x], pall12.at[zz, x], gxs.at[zz], gxr.at[zz], other))

    state = lax.fori_loop(0, 3, newton, (grams, [eye] * 3))
    forward(1)
    forward(3)
    state = lax.fori_loop(3, NS_STEPS - 1, newton, state)
    forward(2)
    grams, polys = state
    h_sum = jnp.zeros((R, R), F32)
    for j in range(3):
        poly = 1.5 * polys[j] - 0.5 * dot(grams[j], polys[j])
        turned = dot(mixes[j], poly, 0, 0) * scales[j]
        nall[z, j * R:(j + 1) * R, :] = turned
        h_sum = h_sum + dot(turned, sums[j], 0, 0) * wrows[j]
    hbuf_y[y] = h_sum
    exchange(hbuf_y, hs.at[0], hr.at[0], y, "y", "send")
    exchange(nall, ns, nr, z, "z", "send")

    def second(k, proj):
        acc = jnp.zeros((R, WIDTH), F32)
        for h in range(2):
            high, low = halves(slab[k, h * HALF:(h + 1) * HALF, :])
            acc = acc + three(proj(h), high, low)
        high, low = halves(acc)
        at = pl.ds(pl.multiple_of(k * R, R), R)
        yhi[at, :] = high
        ylo[at, :] = low

    def second0(zz):
        second(zz * 3, lambda h: pall0[zz, h])

    def second12(zz):
        col_to(pall12.at[zz, 1 - x], pall12.at[zz, 1 - x], gxs.at[zz], gxr.at[zz], other).wait_recv()

        def one(j, carry):
            second(zz * 3 + 1 + j, lambda h: pall12[zz, h, j])
            return carry

        lax.fori_loop(0, 2, one, 0)

    second0(z)
    second12(z)
    exchange(hbuf_y, hs.at[0], hr.at[0], y, "y", "wait")
    hbuf_z[z] = sum4(hbuf_y)
    exchange(hbuf_z, hs.at[1], hr.at[1], z, "z", "send")
    exchange(pall0, g0s, g0r, z, "z", "wait")

    def rest0(d, carry):
        second0(z_plus(d))
        return carry

    lax.fori_loop(1, 4, rest0, 0)
    exchange(hbuf_z, hs.at[1], hr.at[1], z, "z", "wait")
    hbuf_q[q] = sum4(hbuf_z)
    exchange(hbuf_q, hs.at[2], hr.at[2], q, "q", "send")
    for d in (1, 3, 2):
        second12(z_plus(d))
    exchange(nall, ns, nr, z, "z", "wait")
    exchange(hbuf_q, hs.at[2], hr.at[2], q, "q", "wait")
    h_terms = sum4(hbuf_q)

    core_t = dot(inv1[...], h_terms, 1, 1)
    core_t = core_t * lax.rsqrt(jnp.sum(core_t * core_t, axis=1, keepdims=True) + 1e-06)
    core_gram = dot(core_t, core_t, 1, 1)
    stacked = nall[...].reshape(SLICES * R, R)
    mixed = dot(core_t, stacked, 1, 1)
    k_of, s_of = iotas((SLICES, SLICES * R))
    spread = jnp.where(s_of // R == k_of, 1.0, 0.0)
    weighted = mixed * dot(weight, spread, 0, 0)
    v_local = three(weighted, yhi[...], ylo[...])
    for i in range(CUTS):
        part = v_local[(i // 8) * 32:(i // 8) * 32 + 32, (i % 8) * 128:(i % 8) * 128 + 128]
        vsend[i] = part
    vrecv[c] = vsend[c]
    for d in range(1, CUTS):
        to = cuts_at(d)
        send(cuts_to(vsend.at[to], vrecv.at[c], vs.at[to], vr.at[c], to))
    core_out[...] = dot(eye, core_t, 1, 1) * 8.0
    gram_out[...] = core_gram
    inv2 = inverse(sum4(sgbuf_q) * core_gram)
    for d in range(1, CUTS):
        frm = cuts_at(d)
        cuts_to(vsend.at[frm], vrecv.at[frm], vs.at[frm], vr.at[frm], frm).wait_recv()
    total = vrecv[0]
    for i in range(1, CUTS):
        total = total + vrecv[i]
    vfull[c] = total
    for d in range(1, CUTS):
        to = cuts_at(d)
        send(cuts_to(vfull.at[c], vfull.at[c], as_.at[to], ar.at[c], to))
    for d in range(1, CUTS):
        frm = cuts_at(d)
        cuts_to(vfull.at[frm], vfull.at[frm], as_.at[frm], ar.at[frm], frm).wait_recv()
    v_terms = jnp.concatenate(
        [jnp.concatenate([vfull[i * 8 + b] for b in range(8)], axis=1) for i in range(2)], axis=0
    )
    vt = dot(inv2, v_terms)
    fbuf[l, :R, :] = dot(vt, vt, 1, 1)
    found = mixed * three(vt, yhi[...], ylo[...], 1)
    fbuf[l, R:, :] = jnp.concatenate([dot(spread, found, 1, 1), jnp.zeros((4, R), F32)], axis=0)
    for d in range(1, COL):
        to = col_at(d)
        send(col_to(fbuf.at[l], fbuf.at[l], fs.at[to], fr.at[l], to))
    vt_out[...] = vt
    for d in range(1, COL):
        frm = col_at(d)
        col_to(fbuf.at[frm], fbuf.at[frm], fs.at[frm], fr.at[frm], frm).wait_recv()
    total = fbuf[0]
    for i in range(1, COL):
        total = total + fbuf[i]
    total_out[...] = total

    for copy in sent:
        copy.wait_send()


def finish(total_ref, vt_ref, core_t_ref, gram_ref, core_out, column_out, weight_out):
    total = total_ref[...]
    v_gram = total[:R]
    w_terms = total[R:R + SLICES]
    d_row, d_col = diagonals(v_gram)
    n_row, n_col = lax.rsqrt(d_row + 1e-06), lax.rsqrt(d_col + 1e-06)
    core_out[...] = core_t_ref[...]
    column_out[...] = vt_ref[...] * (n_col * (8192.0 ** 0.5))
    inv3 = inverse(gram_ref[...] * (v_gram * n_col * n_row))
    weight_out[...] = dot(w_terms * n_row, inv3)


def shards(records, row_lengths, row_mask, core_init, column_init, weight_init):
    vmem = pl.BlockSpec(memory_space=pltpu.VMEM)
    dma = pltpu.SemaphoreType.DMA
    four = dma((4,))
    chunk = pltpu.VMEM((4, 2, R, HALF), F32)
    square = jax.ShapeDtypeStruct((R, R), F32)
    found = pl.pallas_call(
        kernel,
        out_shape=(
            jax.ShapeDtypeStruct((80, R), F32),
            jax.ShapeDtypeStruct((R, WIDTH), F32),
            square,
            square,
        ),
        in_specs=[pl.BlockSpec(memory_space=pltpu.SMEM), pl.BlockSpec(memory_space=pl.ANY)] + [vmem] * 4,
        out_specs=(vmem,) * 4,
        scratch_shapes=[
            pltpu.VMEM((SLICES, SLOTS, WIDTH), F32),
            pltpu.VMEM((SLICES, SLOTS), F32),
            chunk, chunk, chunk,
            chunk, chunk, chunk, chunk,
            pltpu.VMEM((2, R, HALF), F32),
            pltpu.VMEM((2, R, HALF), F32),
            chunk,
            pltpu.VMEM((4, 2, 2, R, HALF), F32),
            pltpu.VMEM((2, 2, R, R), F32),
            pltpu.VMEM((4, 3 * R, R), F32),
            pltpu.VMEM((SLICES * R, WIDTH), BF16),
            pltpu.VMEM((SLICES * R, WIDTH), BF16),
            pltpu.VMEM((4, R, R), F32),
            pltpu.VMEM((4, R, R), F32),
            pltpu.VMEM((4, R, R), F32),
            pltpu.VMEM((2, R, R), F32),
            pltpu.VMEM((4, R, R), F32),
            pltpu.VMEM((4, R, R), F32),
            pltpu.VMEM((4, R, R), F32),
            pltpu.VMEM((CUTS, 32, 128), F32),
            pltpu.VMEM((CUTS, 32, 128), F32),
            pltpu.VMEM((CUTS, 32, 128), F32),
            pltpu.VMEM((COL, 80, R), F32),
            pltpu.VMEM((R, R), F32),
            dma((SLICES,)),
            four, four, four, four, four, four,
            dma, dma,
            dma, dma((2,)),
            four, four, four, four, four, four,
            four, four,
            dma((2, 4)), dma((2, 4)),
            dma((5,)), dma((5,)),
            dma((3, 4)), dma((3, 4)),
            dma((CUTS,)), dma((CUTS,)),
            dma((CUTS,)), dma((CUTS,)),
            dma((COL,)), dma((COL,)),
        ],
        compiler_params=pltpu.CompilerParams(
            collective_id=0, has_side_effects=True, vmem_limit_bytes=60 * 1024 * 1024
        ),
    )(row_lengths, records, row_mask, core_init, column_init, weight_init)
    return pl.pallas_call(
        finish,
        out_shape=(
            square,
            jax.ShapeDtypeStruct((R, WIDTH), F32),
            jax.ShapeDtypeStruct((SLICES, R), F32),
        ),
        in_specs=[vmem] * 4,
        out_specs=(vmem,) * 3,
    )(*found)


def solution(mesh):
    in_specs = (
        P("cuts", None, "col"),
        P("cuts"),
        P("cuts", None),
        P(),
        P(None, "col"),
        P("cuts", None),
    )
    out_specs = (P(), P(None, "col"), P("cuts", None))
    return jax.shard_map(shards, mesh=mesh, in_specs=in_specs, out_specs=out_specs, check_vma=False)
```

```python
import functools

import jax
import jax.numpy as jnp
from jax import lax
from jax.experimental import pallas as pl
from jax.experimental.pallas import tpu as pltpu
from jax.sharding import PartitionSpec as P

R = 64
NS_STEPS = 8
CUTS = 16
COL = 8
SLICES = 12
SLOTS = 512
WIDTH = 1024
HALF = 256

F32 = jnp.float32
BF16 = jnp.bfloat16
HP = lax.Precision.HIGHEST
MESH = pl.DeviceIdType.MESH


def dot(a, b, ca=1, cb=0, precision=HP):
    return lax.dot_general(
        a, b, (((ca,), (cb,)), ((), ())), precision=precision, preferred_element_type=F32
    )


def fast(a, b, ca=1, cb=0):
    return dot(a, b, ca, cb, lax.Precision.DEFAULT)


def halves(x):
    high = x.astype(BF16)
    return high, (x - high.astype(F32)).astype(BF16)


def three(a, b_high, b_low, cb=0):
    a_high, a_low = halves(a)
    rows = a.shape[0]
    both = fast(jnp.concatenate([a_high, a_low], axis=0), b_high, 1, cb)
    return both[:rows] + both[rows:] + fast(a_high, b_low, 1, cb)


def iotas(shape):
    return lax.broadcasted_iota(jnp.int32, shape, 0), lax.broadcasted_iota(jnp.int32, shape, 1)


def pack(a):
    half = a.shape[0] // 2
    return jnp.concatenate([a[:half], a[half:]], axis=1)


def unpack(a):
    return jnp.concatenate([a[:, :R], a[:, R:]], axis=0)


def diagonals(a):
    rows, cols = iotas(a.shape)
    kept = jnp.where(rows == cols, a, 0.0)
    return jnp.sum(kept, axis=0, keepdims=True), jnp.sum(kept, axis=1, keepdims=True)


def inverse(gram):
    rows, cols = iotas(gram.shape)
    d_row, d_col = diagonals(gram)
    s_row, s_col = lax.rsqrt(d_row), lax.rsqrt(d_col)

    def sweep(t, a):
        at = [4 * t + i for i in range(4)]
        r = [jnp.sum(jnp.where(rows == p, a, 0.0), axis=0, keepdims=True) for p in at]
        c = [jnp.sum(jnp.where(cols == p, a, 0.0), axis=1, keepdims=True) for p in at]

        def pivot(m, n):
            return jnp.sum(jnp.where(rows[:, :1] == at[m], c[n], 0.0), axis=0, keepdims=True)

        a00, a01, a11 = pivot(0, 0), pivot(0, 1), pivot(1, 1)
        b00, b01, b10, b11 = pivot(0, 2), pivot(0, 3), pivot(1, 2), pivot(1, 3)
        k = 1.0 / (a00 * a11 - a01 * a01)
        i00, i01, i11 = a11 * k, -a01 * k, a00 * k
        t00, t01 = i00 * b00 + i01 * b10, i00 * b01 + i01 * b11
        t10, t11 = i01 * b00 + i11 * b10, i01 * b01 + i11 * b11
        s0 = pivot(2, 2) - (b00 * t00 + b10 * t10)
        s1 = pivot(2, 3) - (b00 * t01 + b10 * t11)
        s2 = pivot(3, 3) - (b01 * t01 + b11 * t11)
        m = 1.0 / (s0 * s2 - s1 * s1)
        r = [v + jnp.where(cols[:1] == p, 1.0, 0.0) for v, p in zip(r, at)]
        c = [v - jnp.where(rows[:, :1] == p, 1.0, 0.0) for v, p in zip(c, at)]
        y0, y1 = i00 * r[0] + i01 * r[1], i01 * r[0] + i11 * r[1]
        z0, z1 = r[2] - (b00 * y0 + b10 * y1), r[3] - (b01 * y0 + b11 * y1)
        u2, u3 = (s2 * m) * z0 - (s1 * m) * z1, (s0 * m) * z1 - (s1 * m) * z0
        u0, u1 = y0 - (t00 * u2 + t01 * u3), y1 - (t10 * u2 + t11 * u3)
        return a - ((c[0] * u0 + c[1] * u1) + (c[2] * u2 + c[3] * u3))

    return lax.fori_loop(0, R // 4, sweep, gram * s_col * s_row) * s_col * s_row


def kernel(
    len_ref, rec_ref, mask_ref, core_ref, column_ref, weight_ref,
    total_out, vt_out, core_out, gram_out,
    slab, vmask, keep, xsend, xrecv, zsend, zrecv, z0send, z0recv, x0send, x0recv, pall0, pall12,
    sgram, nall, yhi, ylo,
    sgbuf_y, sgbuf_q, cgbuf_z, cgbuf_x, hbuf_y, hbuf_z, hbuf_q, vsend, vrecv, vfull, fbuf, inv1, slice_gram, wide,
    slab_sem, xs, xr, zs, zr, z0s, z0r, x0s, x0r, ss, sr, gxs, gxr, gzs, gzr, g0s, g0r,
    ns, nr, ws, wr, cs, cr, hs, hr, vs, vr, as_, ar, fs, fr,
):
    c = lax.axis_index("cuts")
    l = lax.axis_index("col")
    z, x = l // 2, l % 2
    y, q = c // 4, c % 4
    other = z * 2 + (1 - x)

    sent = []

    def send(copy):
        copy.start()
        sent.append(copy)

    def col_to(src, dst, s, r, where):
        return pltpu.make_async_remote_copy(
            src_ref=src, dst_ref=dst, send_sem=s, recv_sem=r,
            device_id={"col": where}, device_id_type=MESH,
        )

    def cuts_to(src, dst, s, r, where):
        return pltpu.make_async_remote_copy(
            src_ref=src, dst_ref=dst, send_sem=s, recv_sem=r,
            device_id={"cuts": where}, device_id_type=MESH,
        )

    def col_at(d):
        return lax.rem(l + d, COL)

    def cuts_at(d):
        return lax.rem(c + d, CUTS)

    def z_plus(d):
        return lax.rem(z + d, 4)

    def exchange(buf, s, r, here, axis, stage):
        for d in (2, 1, 3):
            there = lax.rem(here + d, 4)
            if axis == "z":
                go, to = col_to, there * 2 + x
            else:
                go, to = cuts_to, (there * 4 + q if axis == "y" else y * 4 + there)
            if stage == "send":
                send(go(buf.at[here], buf.at[here], s.at[there], r.at[here], to))
            else:
                go(buf.at[there], buf.at[there], s.at[there], r.at[there], to).wait_recv()

    def sum4(buf):
        return (buf[0] + buf[1]) + (buf[2] + buf[3])

    def slab_copy(k):
        return pltpu.make_async_copy(rec_ref.at[k], slab.at[k], slab_sem.at[k])

    far = (2, 1, 3, 0)
    for d, j in ((2, 0), (2, 1), (2, 2), (1, 1), (1, 2), (1, 0), (3, 1), (3, 2), (3, 0), (0, 1), (0, 2), (0, 0)):
        slab_copy(z_plus(d) * 3 + j).start()

    barrier = pltpu.get_barrier_semaphore()
    pl.semaphore_signal(barrier, inc=1, device_id={"col": other}, device_id_type=MESH)
    for d in range(1, 4):
        for axis, to in (
            ("col", z_plus(d) * 2 + x),
            ("cuts", lax.rem(y + d, 4) * 4 + q),
            ("cuts", y * 4 + lax.rem(q + d, 4)),
        ):
            pl.semaphore_signal(barrier, inc=1, device_id={axis: to}, device_id_type=MESH)

    slot = lax.broadcasted_iota(jnp.int32, (1, SLOTS), 1)
    for k in range(SLICES):
        vmask[k:k + 1, :] = jnp.where((slot < len_ref[k]) & (mask_ref[k:k + 1, :] == 1), 1.0, 0.0)
    weight = weight_ref[...]
    column = column_ref[...]
    c_high, c_low = halves(column)
    c_both = jnp.concatenate([c_high, c_low], axis=0)
    cgbuf_z[z] = pack(dot(column, column, 1, 1))
    sgbuf_y[y] = pack(dot(weight, weight, 0, 0))

    def part_of(k, h):
        high, low = halves(slab[k, pl.ds(pl.multiple_of(h * HALF, HALF), HALF), :])
        both = fast(c_both, high, 1, 1)
        return both[:R] + both[R:] + fast(c_high, low, 1, 1)

    def pair(zz):
        def one(j, carry):
            k = zz * 3 + 1 + j
            slab_copy(k).wait()
            xsend[zz, j] = part_of(k, 1 - x)
            keep[zz, j] = part_of(k, x)
            return carry

        lax.fori_loop(0, 2, one, 0)

    def pair_send(zz):
        send(col_to(xsend.at[zz], xrecv.at[zz], xs.at[zz], xr.at[zz], other))

    def pair_sum(zz):
        col_to(xsend.at[zz], xrecv.at[zz], xs.at[zz], xr.at[zz], other).wait_recv()
        zsend[zz] = keep[zz] + xrecv[zz]

    def pair_pass(zz):
        pair_sum(zz)
        send(col_to(zsend.at[zz], zrecv.at[z], zs.at[zz], zr.at[z], zz * 2 + x))

    def single(zz):
        slab_copy(zz * 3).wait()

        def one(h, carry):
            z0send[zz, h] = part_of(zz * 3, h)
            return carry

        lax.fori_loop(0, 2, one, 0)

    def single_send(zz):
        send(col_to(z0send.at[zz], z0recv.at[z], z0s.at[zz], z0r.at[z], zz * 2 + x))

    single(z_plus(2))
    pl.semaphore_wait(barrier, 10)
    single_send(z_plus(2))
    pair(z_plus(2))
    pair_send(z_plus(2))
    exchange(sgbuf_y, ws.at[0], wr.at[0], y, "y", "send")
    exchange(cgbuf_z, cs, cr, z, "z", "send")
    pair(z_plus(1))
    pair_send(z_plus(1))
    single(z_plus(1))
    single_send(z_plus(1))
    pair_pass(z_plus(2))
    pair(z_plus(3))
    pair_send(z_plus(3))
    exchange(sgbuf_y, ws.at[0], wr.at[0], y, "y", "wait")
    sgbuf_q[q] = sum4(sgbuf_y)
    exchange(sgbuf_q, ws.at[1], wr.at[1], q, "q", "send")
    single(z_plus(3))
    single_send(z_plus(3))
    pair_pass(z_plus(1))
    exchange(cgbuf_z, cs, cr, z, "z", "wait")
    cgbuf_x[x] = sum4(cgbuf_z)
    send(col_to(cgbuf_x.at[x], cgbuf_x.at[x], cs.at[4], cr.at[4], other))
    pair(z)
    pair_send(z)
    single(z)
    pair_pass(z_plus(3))
    for d in far[:3]:
        zz = z_plus(d)
        col_to(z0send.at[zz], z0recv.at[zz], z0s.at[zz], z0r.at[zz], zz * 2 + x).wait_recv()
    x0send[...] = (z0send[z] + z0recv[z_plus(1)]) + (z0recv[z_plus(2)] + z0recv[z_plus(3)])
    send(col_to(x0send, x0recv, x0s, x0r, other))
    pair_sum(z)

    def mask_of(j, h):
        return vmask[pl.ds(z * 3 + j, 1), pl.ds(pl.multiple_of(h * HALF, HALF), HALF)]

    for d in far[:3]:
        zz = z_plus(d)
        col_to(zsend.at[zz], zrecv.at[zz], zs.at[zz], zr.at[zz], zz * 2 + x).wait_recv()
    partial_grams = []
    for j in range(2):
        total = (zsend[z, j] + zrecv[z_plus(1), j]) + (zrecv[z_plus(2), j] + zrecv[z_plus(3), j])
        total = total * mask_of(1 + j, x)
        pall12[z, x, j] = total
        partial_grams.append(dot(total, total, 1, 1))
    sgram[x] = jnp.concatenate(partial_grams, axis=1)
    send(col_to(sgram.at[x], sgram.at[x], ss, sr.at[x], other))
    for d in (1, 3, 2):
        zz = z_plus(d)
        send(col_to(pall12.at[z, x], pall12.at[z, x], gzs.at[zz], gzr.at[z], zz * 2 + x))
    send(col_to(pall12.at[z, x], pall12.at[z, x], gxs.at[z], gxr.at[z], other))

    exchange(sgbuf_q, ws.at[1], wr.at[1], q, "q", "wait")
    slice_gram[...] = unpack(sum4(sgbuf_q))
    col_to(cgbuf_x.at[1 - x], cgbuf_x.at[1 - x], cs.at[4], cr.at[4], other).wait_recv()
    inv1[...] = inverse(slice_gram[...] * unpack(cgbuf_x[0] + cgbuf_x[1]))
    k_of, s_of = iotas((SLICES, SLICES * R))
    spread = jnp.where(s_of // R == k_of, 1.0, 0.0)
    wide[...] = dot(weight, spread, 0, 0)
    col_to(x0send, x0recv, x0s, x0r, other).wait_recv()
    gram0 = jnp.zeros((R, R), F32)
    for h in range(2):
        total = (x0send[h] + x0recv[h]) * mask_of(0, h)
        pall0[z, h] = total
        gram0 = gram0 + dot(total, total, 1, 1)
    for d in far[:3]:
        zz = z_plus(d)
        send(col_to(pall0.at[z], pall0.at[z], g0s.at[zz], g0r.at[z], zz * 2 + x))
    col_to(sgram.at[1 - x], sgram.at[1 - x], ss, sr.at[1 - x], other).wait_recv()

    rows, cols = iotas((R, R))
    eye = jnp.where(rows == cols, 1.0, 0.0)
    both = sgram[0] + sgram[1]
    sums = [gram0, both[:, :R], both[:, R:]]
    grams, mixes, scales, wrows = [], [], [], []
    for j in range(3):
        wrow = weight_ref[pl.ds(z * 3 + j, 1), :]
        mix = core_ref[...] * wrow
        g = dot(dot(mix, sums[j]), mix, 1, 1)
        trace = jnp.sum(jnp.where(rows == cols, g, 0.0), axis=(0, 1), keepdims=True) + 1e-06
        grams.append(g / trace)
        mixes.append(mix)
        scales.append(lax.rsqrt(trace))
        wrows.append(wrow)

    def newton(_, carry):
        gs_, ps_ = carry
        next_g, next_p = [], []
        for g, p in zip(gs_, ps_):
            square = dot(g, g)
            next_p.append(1.5 * p - 0.5 * dot(g, p))
            next_g.append(2.25 * g - 1.5 * square + 0.25 * dot(square, g))
        return next_g, next_p

    def forward(d):
        zz = z_plus(d)
        col_to(pall12.at[zz, x], pall12.at[zz, x], gzs.at[zz], gzr.at[zz], zz * 2 + x).wait_recv()
        send(col_to(pall12.at[zz, x], pall12.at[zz, x], gxs.at[zz], gxr.at[zz], other))

    state = lax.fori_loop(0, 3, newton, (grams, [eye] * 3))
    forward(1)
    forward(3)
    state = lax.fori_loop(3, NS_STEPS - 1, newton, state)
    forward(2)
    grams, polys = state
    h_sum = jnp.zeros((R, R), F32)
    turned_all = []
    for j in range(3):
        poly = 1.5 * polys[j] - 0.5 * dot(grams[j], polys[j])
        turned = dot(mixes[j], poly, 0, 0) * scales[j]
        turned_all.append(turned)
        h_sum = h_sum + dot(turned, sums[j], 0, 0) * wrows[j]
    hbuf_y[y] = pack(h_sum)
    nall[z] = pack(jnp.concatenate(turned_all, axis=0))
    exchange(hbuf_y, hs.at[0], hr.at[0], y, "y", "send")
    exchange(nall, ns, nr, z, "z", "send")

    def second(k, proj):
        acc = jnp.zeros((R, WIDTH), F32)
        for h in range(2):
            high, low = halves(slab[k, h * HALF:(h + 1) * HALF, :])
            acc = acc + three(proj(h), high, low)
        high, low = halves(acc)
        at = pl.ds(pl.multiple_of(k * R, R), R)
        yhi[at, :] = high
        ylo[at, :] = low

    def second0(zz):
        second(zz * 3, lambda h: pall0[zz, h])

    def second12(zz):
        col_to(pall12.at[zz, 1 - x], pall12.at[zz, 1 - x], gxs.at[zz], gxr.at[zz], other).wait_recv()

        def one(j, carry):
            second(zz * 3 + 1 + j, lambda h: pall12[zz, h, j])
            return carry

        lax.fori_loop(0, 2, one, 0)

    exchange(pall0, g0s, g0r, z, "z", "wait")

    def all0(zz, carry):
        second0(zz)
        return carry

    lax.fori_loop(0, 4, all0, 0)
    second12(z)
    exchange(hbuf_y, hs.at[0], hr.at[0], y, "y", "wait")
    hbuf_z[z] = sum4(hbuf_y)
    exchange(hbuf_z, hs.at[1], hr.at[1], z, "z", "send")
    second12(z_plus(1))
    exchange(hbuf_z, hs.at[1], hr.at[1], z, "z", "wait")
    hbuf_q[q] = sum4(hbuf_z)
    exchange(hbuf_q, hs.at[2], hr.at[2], q, "q", "send")
    second12(z_plus(3))
    second12(z_plus(2))
    exchange(nall, ns, nr, z, "z", "wait")
    exchange(hbuf_q, hs.at[2], hr.at[2], q, "q", "wait")
    h_terms = unpack(sum4(hbuf_q))

    core_t = dot(inv1[...], h_terms, 1, 1)
    core_t = core_t * lax.rsqrt(jnp.sum(core_t * core_t, axis=1, keepdims=True) + 1e-06)
    core_gram = dot(core_t, core_t, 1, 1)
    stacked = jnp.concatenate([unpack(nall[i]) for i in range(4)], axis=0)
    mixed = dot(core_t, stacked, 1, 1)
    weighted = mixed * wide[...]
    v_local = three(weighted, yhi[...], ylo[...])
    for i in range(CUTS):
        part = v_local[(i // 8) * 32:(i // 8) * 32 + 32, (i % 8) * 128:(i % 8) * 128 + 128]
        vsend[i] = part
    vrecv[c] = vsend[c]
    for d in range(1, CUTS):
        to = cuts_at(d)
        send(cuts_to(vsend.at[to], vrecv.at[c], vs.at[to], vr.at[c], to))
    core_out[...] = dot(eye, core_t, 1, 1) * 8.0
    gram_out[...] = core_gram
    inv2 = inverse(slice_gram[...] * core_gram)
    for d in range(1, CUTS):
        frm = cuts_at(d)
        cuts_to(vsend.at[frm], vrecv.at[frm], vs.at[frm], vr.at[frm], frm).wait_recv()
    total = vrecv[0]
    for i in range(1, CUTS):
        total = total + vrecv[i]
    vfull[c] = total
    for d in range(1, CUTS):
        to = cuts_at(d)
        send(cuts_to(vfull.at[c], vfull.at[c], as_.at[to], ar.at[c], to))
    for d in range(1, CUTS):
        frm = cuts_at(d)
        cuts_to(vfull.at[frm], vfull.at[frm], as_.at[frm], ar.at[frm], frm).wait_recv()
    v_terms = jnp.concatenate(
        [jnp.concatenate([vfull[i * 8 + b] for b in range(8)], axis=1) for i in range(2)], axis=0
    )
    vt = dot(inv2, v_terms)
    v_gram = dot(vt, vt, 1, 1)
    found = mixed * three(vt, yhi[...], ylo[...], 1)
    w_terms = jnp.concatenate([dot(spread, found, 1, 1), jnp.zeros((4, R), F32)], axis=0)
    fbuf[l] = jnp.concatenate([pack(v_gram), pack(w_terms)], axis=0)
    for d in range(1, COL):
        to = col_at(d)
        send(col_to(fbuf.at[l], fbuf.at[l], fs.at[to], fr.at[l], to))
    vt_out[...] = vt
    for d in range(1, COL):
        frm = col_at(d)
        col_to(fbuf.at[frm], fbuf.at[frm], fs.at[frm], fr.at[frm], frm).wait_recv()
    total = fbuf[0]
    for i in range(1, COL):
        total = total + fbuf[i]
    total_out[...] = total

    for copy in sent:
        copy.wait_send()


def finish(total_ref, vt_ref, core_t_ref, gram_ref, core_out, column_out, weight_out):
    total = total_ref[...]
    v_gram = unpack(total[:32])
    w_terms = unpack(total[32:])[:SLICES]
    d_row, d_col = diagonals(v_gram)
    n_row, n_col = lax.rsqrt(d_row + 1e-06), lax.rsqrt(d_col + 1e-06)
    core_out[...] = core_t_ref[...]
    column_out[...] = vt_ref[...] * (n_col * (8192.0 ** 0.5))
    inv3 = inverse(gram_ref[...] * (v_gram * n_col * n_row))
    weight_out[...] = dot(w_terms * n_row, inv3)


def shards(records, row_lengths, row_mask, core_init, column_init, weight_init):
    vmem = pl.BlockSpec(memory_space=pltpu.VMEM)
    dma = pltpu.SemaphoreType.DMA
    four = dma((4,))
    chunk = pltpu.VMEM((4, 2, R, HALF), F32)
    square = jax.ShapeDtypeStruct((R, R), F32)
    found = pl.pallas_call(
        kernel,
        out_shape=(
            jax.ShapeDtypeStruct((40, 128), F32),
            jax.ShapeDtypeStruct((R, WIDTH), F32),
            square,
            square,
        ),
        in_specs=[pl.BlockSpec(memory_space=pltpu.SMEM), pl.BlockSpec(memory_space=pl.ANY)] + [vmem] * 4,
        out_specs=(vmem,) * 4,
        scratch_shapes=[
            pltpu.VMEM((SLICES, SLOTS, WIDTH), F32),
            pltpu.VMEM((SLICES, SLOTS), F32),
            chunk, chunk, chunk,
            chunk, chunk, chunk, chunk,
            pltpu.VMEM((2, R, HALF), F32),
            pltpu.VMEM((2, R, HALF), F32),
            chunk,
            pltpu.VMEM((4, 2, 2, R, HALF), F32),
            pltpu.VMEM((2, R, 128), F32),
            pltpu.VMEM((4, 3 * R // 2, 128), F32),
            pltpu.VMEM((SLICES * R, WIDTH), BF16),
            pltpu.VMEM((SLICES * R, WIDTH), BF16),
            pltpu.VMEM((4, 32, 128), F32),
            pltpu.VMEM((4, 32, 128), F32),
            pltpu.VMEM((4, 32, 128), F32),
            pltpu.VMEM((2, 32, 128), F32),
            pltpu.VMEM((4, 32, 128), F32),
            pltpu.VMEM((4, 32, 128), F32),
            pltpu.VMEM((4, 32, 128), F32),
            pltpu.VMEM((CUTS, 32, 128), F32),
            pltpu.VMEM((CUTS, 32, 128), F32),
            pltpu.VMEM((CUTS, 32, 128), F32),
            pltpu.VMEM((COL, 40, 128), F32),
            pltpu.VMEM((R, R), F32),
            pltpu.VMEM((R, R), F32),
            pltpu.VMEM((R, SLICES * R), F32),
            dma((SLICES,)),
            four, four, four, four, four, four,
            dma, dma,
            dma, dma((2,)),
            four, four, four, four, four, four,
            four, four,
            dma((2, 4)), dma((2, 4)),
            dma((5,)), dma((5,)),
            dma((3, 4)), dma((3, 4)),
            dma((CUTS,)), dma((CUTS,)),
            dma((CUTS,)), dma((CUTS,)),
            dma((COL,)), dma((COL,)),
        ],
        compiler_params=pltpu.CompilerParams(
            collective_id=0, has_side_effects=True, vmem_limit_bytes=60 * 1024 * 1024
        ),
    )(row_lengths, records, row_mask, core_init, column_init, weight_init)
    return pl.pallas_call(
        finish,
        out_shape=(
            square,
            jax.ShapeDtypeStruct((R, WIDTH), F32),
            jax.ShapeDtypeStruct((SLICES, R), F32),
        ),
        in_specs=[vmem] * 4,
        out_specs=(vmem,) * 3,
    )(*found)


def solution(mesh):
    in_specs = (
        P("cuts", None, "col"),
        P("cuts"),
        P("cuts", None),
        P(),
        P(None, "col"),
        P("cuts", None),
    )
    out_specs = (P(), P(None, "col"), P("cuts", None))
    return jax.shard_map(shards, mesh=mesh, in_specs=in_specs, out_specs=out_specs, check_vma=False)
```

```python
import functools

import jax
import jax.numpy as jnp
from jax import lax
from jax.experimental import pallas as pl
from jax.experimental.pallas import tpu as pltpu
from jax.sharding import PartitionSpec as P

R = 64
NS_STEPS = 8
CUTS = 16
COL = 8
SLICES = 12
SLOTS = 512
WIDTH = 1024
HALF = 256

F32 = jnp.float32
BF16 = jnp.bfloat16
HP = lax.Precision.HIGHEST
MESH = pl.DeviceIdType.MESH


def dot(a, b, ca=1, cb=0, precision=HP):
    return lax.dot_general(
        a, b, (((ca,), (cb,)), ((), ())), precision=precision, preferred_element_type=F32
    )


def fast(a, b, ca=1, cb=0):
    return dot(a, b, ca, cb, lax.Precision.DEFAULT)


def halves(x):
    high = x.astype(BF16)
    return high, (x - high.astype(F32)).astype(BF16)


def three(a, b_high, b_low, cb=0):
    a_high, a_low = halves(a)
    rows = a.shape[0]
    both = fast(jnp.concatenate([a_high, a_low], axis=0), b_high, 1, cb)
    return both[:rows] + both[rows:] + fast(a_high, b_low, 1, cb)


def iotas(shape):
    return lax.broadcasted_iota(jnp.int32, shape, 0), lax.broadcasted_iota(jnp.int32, shape, 1)


def pack(a):
    half = a.shape[0] // 2
    return jnp.concatenate([a[:half], a[half:]], axis=1)


def unpack(a):
    return jnp.concatenate([a[:, :R], a[:, R:]], axis=0)


def diagonals(a):
    rows, cols = iotas(a.shape)
    kept = jnp.where(rows == cols, a, 0.0)
    return jnp.sum(kept, axis=0, keepdims=True), jnp.sum(kept, axis=1, keepdims=True)


def inverse(gram):
    rows, cols = iotas(gram.shape)
    d_row, d_col = diagonals(gram)
    s_row, s_col = lax.rsqrt(d_row), lax.rsqrt(d_col)

    def sweep(t, a):
        at = [4 * t + i for i in range(4)]
        r = [jnp.sum(jnp.where(rows == p, a, 0.0), axis=0, keepdims=True) for p in at]
        c = [jnp.sum(jnp.where(cols == p, a, 0.0), axis=1, keepdims=True) for p in at]

        def pivot(m, n):
            return jnp.sum(jnp.where(rows[:, :1] == at[m], c[n], 0.0), axis=0, keepdims=True)

        a00, a01, a11 = pivot(0, 0), pivot(0, 1), pivot(1, 1)
        b00, b01, b10, b11 = pivot(0, 2), pivot(0, 3), pivot(1, 2), pivot(1, 3)
        k = 1.0 / (a00 * a11 - a01 * a01)
        i00, i01, i11 = a11 * k, -a01 * k, a00 * k
        t00, t01 = i00 * b00 + i01 * b10, i00 * b01 + i01 * b11
        t10, t11 = i01 * b00 + i11 * b10, i01 * b01 + i11 * b11
        s0 = pivot(2, 2) - (b00 * t00 + b10 * t10)
        s1 = pivot(2, 3) - (b00 * t01 + b10 * t11)
        s2 = pivot(3, 3) - (b01 * t01 + b11 * t11)
        m = 1.0 / (s0 * s2 - s1 * s1)
        r = [v + jnp.where(cols[:1] == p, 1.0, 0.0) for v, p in zip(r, at)]
        c = [v - jnp.where(rows[:, :1] == p, 1.0, 0.0) for v, p in zip(c, at)]
        y0, y1 = i00 * r[0] + i01 * r[1], i01 * r[0] + i11 * r[1]
        z0, z1 = r[2] - (b00 * y0 + b10 * y1), r[3] - (b01 * y0 + b11 * y1)
        u2, u3 = (s2 * m) * z0 - (s1 * m) * z1, (s0 * m) * z1 - (s1 * m) * z0
        u0, u1 = y0 - (t00 * u2 + t01 * u3), y1 - (t10 * u2 + t11 * u3)
        return a - ((c[0] * u0 + c[1] * u1) + (c[2] * u2 + c[3] * u3))

    return lax.fori_loop(0, R // 4, sweep, gram * s_col * s_row) * s_col * s_row


def kernel(
    len_ref, rec_ref, mask_ref, core_ref, column_ref, weight_ref,
    total_out, vt_out, core_out, gram_out,
    slab, vmask, keep, xsend, xrecv, zsend, zrecv, z0send, z0recv, x0send, x0recv, pall0, pall12,
    sgram, nall, yhi, ylo,
    sgbuf_y, sgbuf_q, cgbuf_z, cgbuf_x, hbuf_y, hbuf_z, hbuf_q, vsend, vrecv, vfull, fbuf, inv1, slice_gram, wide,
    slab_sem, xs, xr, zs, zr, z0s, z0r, x0s, x0r, ss, sr, gxs, gxr, gzs, gzr, g0s, g0r,
    ns, nr, ws, wr, cs, cr, hs, hr, vs, vr, as_, ar, fs, fr,
):
    c = lax.axis_index("cuts")
    l = lax.axis_index("col")
    z, x = l // 2, l % 2
    y, q = c // 4, c % 4
    other = z * 2 + (1 - x)

    sent = []

    def send(copy):
        copy.start()
        sent.append(copy)

    def col_to(src, dst, s, r, where):
        return pltpu.make_async_remote_copy(
            src_ref=src, dst_ref=dst, send_sem=s, recv_sem=r,
            device_id={"col": where}, device_id_type=MESH,
        )

    def cuts_to(src, dst, s, r, where):
        return pltpu.make_async_remote_copy(
            src_ref=src, dst_ref=dst, send_sem=s, recv_sem=r,
            device_id={"cuts": where}, device_id_type=MESH,
        )

    def col_at(d):
        return lax.rem(l + d, COL)

    def cuts_at(d):
        return lax.rem(c + d, CUTS)

    def z_plus(d):
        return lax.rem(z + d, 4)

    def exchange(buf, s, r, here, axis, stage):
        for d in (2, 1, 3):
            there = lax.rem(here + d, 4)
            if axis == "z":
                go, to = col_to, there * 2 + x
            else:
                go, to = cuts_to, (there * 4 + q if axis == "y" else y * 4 + there)
            if stage == "send":
                send(go(buf.at[here], buf.at[here], s.at[there], r.at[here], to))
            else:
                go(buf.at[there], buf.at[there], s.at[there], r.at[there], to).wait_recv()

    def sum4(buf):
        return (buf[0] + buf[1]) + (buf[2] + buf[3])

    def slab_copy(k):
        return pltpu.make_async_copy(rec_ref.at[k], slab.at[k], slab_sem.at[k])

    far = (2, 1, 3, 0)
    for d, j in ((2, 0), (2, 1), (2, 2), (1, 1), (1, 2), (1, 0), (3, 1), (3, 2), (3, 0), (0, 1), (0, 2), (0, 0)):
        slab_copy(z_plus(d) * 3 + j).start()

    barrier = pltpu.get_barrier_semaphore()
    pl.semaphore_signal(barrier, inc=1, device_id={"col": other}, device_id_type=MESH)
    for d in range(1, 4):
        for axis, to in (
            ("col", z_plus(d) * 2 + x),
            ("cuts", lax.rem(y + d, 4) * 4 + q),
            ("cuts", y * 4 + lax.rem(q + d, 4)),
        ):
            pl.semaphore_signal(barrier, inc=1, device_id={axis: to}, device_id_type=MESH)

    slot = lax.broadcasted_iota(jnp.int32, (1, SLOTS), 1)
    for k in range(SLICES):
        vmask[k:k + 1, :] = jnp.where((slot < len_ref[k]) & (mask_ref[k:k + 1, :] == 1), 1.0, 0.0)
    weight = weight_ref[...]
    column = column_ref[...]
    c_high, c_low = halves(column)
    c_both = jnp.concatenate([c_high, c_low], axis=0)
    cgbuf_z[z] = pack(dot(column, column, 1, 1))
    sgbuf_y[y] = pack(dot(weight, weight, 0, 0))

    def part_of(k, h):
        high, low = halves(slab[k, pl.ds(pl.multiple_of(h * HALF, HALF), HALF), :])
        both = fast(c_both, high, 1, 1)
        return both[:R] + both[R:] + fast(c_high, low, 1, 1)

    def pair(zz):
        def one(j, carry):
            k = zz * 3 + 1 + j
            slab_copy(k).wait()
            xsend[zz, j] = part_of(k, 1 - x)
            keep[zz, j] = part_of(k, x)
            return carry

        lax.fori_loop(0, 2, one, 0)

    def pair_send(zz):
        send(col_to(xsend.at[zz], xrecv.at[zz], xs.at[zz], xr.at[zz], other))

    def pair_sum(zz):
        col_to(xsend.at[zz], xrecv.at[zz], xs.at[zz], xr.at[zz], other).wait_recv()
        zsend[zz] = keep[zz] + xrecv[zz]

    def pair_pass(zz):
        pair_sum(zz)
        send(col_to(zsend.at[zz], zrecv.at[z], zs.at[zz], zr.at[z], zz * 2 + x))

    def single(zz):
        slab_copy(zz * 3).wait()

        def one(h, carry):
            z0send[zz, h] = part_of(zz * 3, h)
            return carry

        lax.fori_loop(0, 2, one, 0)

    def single_send(zz):
        send(col_to(z0send.at[zz], z0recv.at[z], z0s.at[zz], z0r.at[z], zz * 2 + x))

    single(z_plus(2))
    pl.semaphore_wait(barrier, 10)
    single_send(z_plus(2))
    pair(z_plus(2))
    pair_send(z_plus(2))
    exchange(sgbuf_y, ws.at[0], wr.at[0], y, "y", "send")
    exchange(cgbuf_z, cs, cr, z, "z", "send")
    pair(z_plus(1))
    pair_send(z_plus(1))
    single(z_plus(1))
    single_send(z_plus(1))
    pair_pass(z_plus(2))
    pair(z_plus(3))
    pair_send(z_plus(3))
    exchange(sgbuf_y, ws.at[0], wr.at[0], y, "y", "wait")
    sgbuf_q[q] = sum4(sgbuf_y)
    exchange(sgbuf_q, ws.at[1], wr.at[1], q, "q", "send")
    single(z_plus(3))
    single_send(z_plus(3))
    pair_pass(z_plus(1))
    exchange(cgbuf_z, cs, cr, z, "z", "wait")
    cgbuf_x[x] = sum4(cgbuf_z)
    send(col_to(cgbuf_x.at[x], cgbuf_x.at[x], cs.at[4], cr.at[4], other))
    pair(z)
    pair_send(z)
    single(z)
    pair_pass(z_plus(3))
    for d in far[:3]:
        zz = z_plus(d)
        col_to(z0send.at[zz], z0recv.at[zz], z0s.at[zz], z0r.at[zz], zz * 2 + x).wait_recv()
    x0send[...] = (z0send[z] + z0recv[z_plus(1)]) + (z0recv[z_plus(2)] + z0recv[z_plus(3)])
    send(col_to(x0send, x0recv, x0s, x0r, other))
    pair_sum(z)

    def mask_of(j, h):
        return vmask[pl.ds(z * 3 + j, 1), pl.ds(pl.multiple_of(h * HALF, HALF), HALF)]

    for d in far[:3]:
        zz = z_plus(d)
        col_to(zsend.at[zz], zrecv.at[zz], zs.at[zz], zr.at[zz], zz * 2 + x).wait_recv()
    partial_grams = []
    for j in range(2):
        total = (zsend[z, j] + zrecv[z_plus(1), j]) + (zrecv[z_plus(2), j] + zrecv[z_plus(3), j])
        total = total * mask_of(1 + j, x)
        pall12[z, x, j] = total
        partial_grams.append(dot(total, total, 1, 1))
    sgram[x] = jnp.concatenate(partial_grams, axis=1)
    send(col_to(sgram.at[x], sgram.at[x], ss, sr.at[x], other))
    for d in (1, 3, 2):
        zz = z_plus(d)
        send(col_to(pall12.at[z, x], pall12.at[z, x], gzs.at[zz], gzr.at[z], zz * 2 + x))
    send(col_to(pall12.at[z, x], pall12.at[z, x], gxs.at[z], gxr.at[z], other))

    exchange(sgbuf_q, ws.at[1], wr.at[1], q, "q", "wait")
    slice_gram[...] = unpack(sum4(sgbuf_q))
    col_to(cgbuf_x.at[1 - x], cgbuf_x.at[1 - x], cs.at[4], cr.at[4], other).wait_recv()
    inv1[...] = inverse(slice_gram[...] * unpack(cgbuf_x[0] + cgbuf_x[1]))
    k_of, s_of = iotas((SLICES, SLICES * R))
    spread = jnp.where(s_of // R == k_of, 1.0, 0.0)
    wide[...] = dot(weight, spread, 0, 0)
    col_to(x0send, x0recv, x0s, x0r, other).wait_recv()
    gram0 = jnp.zeros((R, R), F32)
    for h in range(2):
        total = (x0send[h] + x0recv[h]) * mask_of(0, h)
        pall0[z, h] = total
        gram0 = gram0 + dot(total, total, 1, 1)
    for d in far[:3]:
        zz = z_plus(d)
        send(col_to(pall0.at[z], pall0.at[z], g0s.at[zz], g0r.at[z], zz * 2 + x))
    col_to(sgram.at[1 - x], sgram.at[1 - x], ss, sr.at[1 - x], other).wait_recv()

    rows, cols = iotas((R, R))
    eye = jnp.where(rows == cols, 1.0, 0.0)
    both = sgram[0] + sgram[1]
    sums = [gram0, both[:, :R], both[:, R:]]
    grams, mixes, scales, wrows = [], [], [], []
    for j in range(3):
        wrow = weight_ref[pl.ds(z * 3 + j, 1), :]
        mix = core_ref[...] * wrow
        g = dot(dot(mix, sums[j]), mix, 1, 1)
        trace = jnp.sum(jnp.where(rows == cols, g, 0.0), axis=(0, 1), keepdims=True) + 1e-06
        grams.append(g / trace)
        mixes.append(mix)
        scales.append(lax.rsqrt(trace))
        wrows.append(wrow)

    left = lax.broadcasted_iota(jnp.int32, (1, 2 * R), 1) < R
    by0 = jnp.where(left, 2.25, 1.5)
    by1 = jnp.where(left, 1.5, 0.5)
    by2 = jnp.where(left, 0.25, 0.0)

    def newton(_, states):
        following = []
        for u in states:
            once = dot(u[:, :R], u)
            twice = dot(once[:, :R], u)
            following.append(by0 * u - by1 * once + by2 * twice)
        return following

    def forward(d):
        zz = z_plus(d)
        col_to(pall12.at[zz, x], pall12.at[zz, x], gzs.at[zz], gzr.at[zz], zz * 2 + x).wait_recv()
        send(col_to(pall12.at[zz, x], pall12.at[zz, x], gxs.at[zz], gxr.at[zz], other))

    state = lax.fori_loop(0, 3, newton, [jnp.concatenate([g, eye], axis=1) for g in grams])
    forward(1)
    forward(3)
    state = lax.fori_loop(3, NS_STEPS - 1, newton, state)
    forward(2)
    h_sum = jnp.zeros((R, R), F32)
    turned_all = []
    for j in range(3):
        poly = (1.5 * state[j] - 0.5 * dot(state[j][:, :R], state[j]))[:, R:]
        turned = dot(mixes[j], poly, 0, 0) * scales[j]
        turned_all.append(turned)
        h_sum = h_sum + dot(turned, sums[j], 0, 0) * wrows[j]
    hbuf_y[y] = pack(h_sum)
    nall[z] = pack(jnp.concatenate(turned_all, axis=0))
    exchange(hbuf_y, hs.at[0], hr.at[0], y, "y", "send")
    exchange(nall, ns, nr, z, "z", "send")

    def second(k, proj):
        acc = jnp.zeros((R, WIDTH), F32)
        for h in range(2):
            high, low = halves(slab[k, h * HALF:(h + 1) * HALF, :])
            acc = acc + three(proj(h), high, low)
        high, low = halves(acc)
        at = pl.ds(pl.multiple_of(k * R, R), R)
        yhi[at, :] = high
        ylo[at, :] = low

    def second0(zz):
        second(zz * 3, lambda h: pall0[zz, h])

    def second12(zz):
        col_to(pall12.at[zz, 1 - x], pall12.at[zz, 1 - x], gxs.at[zz], gxr.at[zz], other).wait_recv()

        def one(j, carry):
            second(zz * 3 + 1 + j, lambda h: pall12[zz, h, j])
            return carry

        lax.fori_loop(0, 2, one, 0)

    exchange(pall0, g0s, g0r, z, "z", "wait")

    def all0(zz, carry):
        second0(zz)
        return carry

    lax.fori_loop(0, 4, all0, 0)
    second12(z)
    exchange(hbuf_y, hs.at[0], hr.at[0], y, "y", "wait")
    hbuf_z[z] = sum4(hbuf_y)
    exchange(hbuf_z, hs.at[1], hr.at[1], z, "z", "send")
    second12(z_plus(1))
    exchange(hbuf_z, hs.at[1], hr.at[1], z, "z", "wait")
    hbuf_q[q] = sum4(hbuf_z)
    exchange(hbuf_q, hs.at[2], hr.at[2], q, "q", "send")
    second12(z_plus(3))
    second12(z_plus(2))
    exchange(nall, ns, nr, z, "z", "wait")
    exchange(hbuf_q, hs.at[2], hr.at[2], q, "q", "wait")
    h_terms = unpack(sum4(hbuf_q))

    core_t = dot(inv1[...], h_terms, 1, 1)
    core_t = core_t * lax.rsqrt(jnp.sum(core_t * core_t, axis=1, keepdims=True) + 1e-06)
    core_gram = dot(core_t, core_t, 1, 1)
    stacked = jnp.concatenate([unpack(nall[i]) for i in range(4)], axis=0)
    mixed = dot(core_t, stacked, 1, 1)
    weighted = mixed * wide[...]
    v_local = three(weighted, yhi[...], ylo[...])
    for i in range(CUTS):
        part = v_local[(i // 8) * 32:(i // 8) * 32 + 32, (i % 8) * 128:(i % 8) * 128 + 128]
        vsend[i] = part
    vrecv[c] = vsend[c]
    for d in range(1, CUTS):
        to = cuts_at(d)
        send(cuts_to(vsend.at[to], vrecv.at[c], vs.at[to], vr.at[c], to))
    core_out[...] = dot(eye, core_t, 1, 1) * 8.0
    gram_out[...] = core_gram
    inv2 = inverse(slice_gram[...] * core_gram)
    for d in range(1, CUTS):
        frm = cuts_at(d)
        cuts_to(vsend.at[frm], vrecv.at[frm], vs.at[frm], vr.at[frm], frm).wait_recv()
    total = vrecv[0]
    for i in range(1, CUTS):
        total = total + vrecv[i]
    vfull[c] = total
    for d in range(1, CUTS):
        to = cuts_at(d)
        send(cuts_to(vfull.at[c], vfull.at[c], as_.at[to], ar.at[c], to))
    for d in range(1, CUTS):
        frm = cuts_at(d)
        cuts_to(vfull.at[frm], vfull.at[frm], as_.at[frm], ar.at[frm], frm).wait_recv()
    v_terms = jnp.concatenate(
        [jnp.concatenate([vfull[i * 8 + b] for b in range(8)], axis=1) for i in range(2)], axis=0
    )
    vt = dot(inv2, v_terms)
    v_gram = dot(vt, vt, 1, 1)
    found = mixed * three(vt, yhi[...], ylo[...], 1)
    w_terms = jnp.concatenate([dot(spread, found, 1, 1), jnp.zeros((4, R), F32)], axis=0)
    fbuf[l] = jnp.concatenate([pack(v_gram), pack(w_terms)], axis=0)
    for d in range(1, COL):
        to = col_at(d)
        send(col_to(fbuf.at[l], fbuf.at[l], fs.at[to], fr.at[l], to))
    vt_out[...] = vt
    for d in range(1, COL):
        frm = col_at(d)
        col_to(fbuf.at[frm], fbuf.at[frm], fs.at[frm], fr.at[frm], frm).wait_recv()
    total = fbuf[0]
    for i in range(1, COL):
        total = total + fbuf[i]
    total_out[...] = total

    for copy in sent:
        copy.wait_send()


def finish(total_ref, vt_ref, core_t_ref, gram_ref, core_out, column_out, weight_out):
    total = total_ref[...]
    v_gram = unpack(total[:32])
    w_terms = unpack(total[32:])[:SLICES]
    d_row, d_col = diagonals(v_gram)
    n_row, n_col = lax.rsqrt(d_row + 1e-06), lax.rsqrt(d_col + 1e-06)
    core_out[...] = core_t_ref[...]
    column_out[...] = vt_ref[...] * (n_col * (8192.0 ** 0.5))
    inv3 = inverse(gram_ref[...] * (v_gram * n_col * n_row))
    weight_out[...] = dot(w_terms * n_row, inv3)


def shards(records, row_lengths, row_mask, core_init, column_init, weight_init):
    vmem = pl.BlockSpec(memory_space=pltpu.VMEM)
    dma = pltpu.SemaphoreType.DMA
    four = dma((4,))
    chunk = pltpu.VMEM((4, 2, R, HALF), F32)
    square = jax.ShapeDtypeStruct((R, R), F32)
    found = pl.pallas_call(
        kernel,
        out_shape=(
            jax.ShapeDtypeStruct((40, 128), F32),
            jax.ShapeDtypeStruct((R, WIDTH), F32),
            square,
            square,
        ),
        in_specs=[pl.BlockSpec(memory_space=pltpu.SMEM), pl.BlockSpec(memory_space=pl.ANY)] + [vmem] * 4,
        out_specs=(vmem,) * 4,
        scratch_shapes=[
            pltpu.VMEM((SLICES, SLOTS, WIDTH), F32),
            pltpu.VMEM((SLICES, SLOTS), F32),
            chunk, chunk, chunk,
            chunk, chunk, chunk, chunk,
            pltpu.VMEM((2, R, HALF), F32),
            pltpu.VMEM((2, R, HALF), F32),
            chunk,
            pltpu.VMEM((4, 2, 2, R, HALF), F32),
            pltpu.VMEM((2, R, 128), F32),
            pltpu.VMEM((4, 3 * R // 2, 128), F32),
            pltpu.VMEM((SLICES * R, WIDTH), BF16),
            pltpu.VMEM((SLICES * R, WIDTH), BF16),
            pltpu.VMEM((4, 32, 128), F32),
            pltpu.VMEM((4, 32, 128), F32),
            pltpu.VMEM((4, 32, 128), F32),
            pltpu.VMEM((2, 32, 128), F32),
            pltpu.VMEM((4, 32, 128), F32),
            pltpu.VMEM((4, 32, 128), F32),
            pltpu.VMEM((4, 32, 128), F32),
            pltpu.VMEM((CUTS, 32, 128), F32),
            pltpu.VMEM((CUTS, 32, 128), F32),
            pltpu.VMEM((CUTS, 32, 128), F32),
            pltpu.VMEM((COL, 40, 128), F32),
            pltpu.VMEM((R, R), F32),
            pltpu.VMEM((R, R), F32),
            pltpu.VMEM((R, SLICES * R), F32),
            dma((SLICES,)),
            four, four, four, four, four, four,
            dma, dma,
            dma, dma((2,)),
            four, four, four, four, four, four,
            four, four,
            dma((2, 4)), dma((2, 4)),
            dma((5,)), dma((5,)),
            dma((3, 4)), dma((3, 4)),
            dma((CUTS,)), dma((CUTS,)),
            dma((CUTS,)), dma((CUTS,)),
            dma((COL,)), dma((COL,)),
        ],
        compiler_params=pltpu.CompilerParams(
            collective_id=0, has_side_effects=True, vmem_limit_bytes=60 * 1024 * 1024
        ),
    )(row_lengths, records, row_mask, core_init, column_init, weight_init)
    return pl.pallas_call(
        finish,
        out_shape=(
            square,
            jax.ShapeDtypeStruct((R, WIDTH), F32),
            jax.ShapeDtypeStruct((SLICES, R), F32),
        ),
        in_specs=[vmem] * 4,
        out_specs=(vmem,) * 3,
    )(*found)


def solution(mesh):
    in_specs = (
        P("cuts", None, "col"),
        P("cuts"),
        P("cuts", None),
        P(),
        P(None, "col"),
        P("cuts", None),
    )
    out_specs = (P(), P(None, "col"), P("cuts", None))
    return jax.shard_map(shards, mesh=mesh, in_specs=in_specs, out_specs=out_specs, check_vma=False)
```

```python
import functools

import jax
import jax.numpy as jnp
from jax import lax
from jax.experimental import pallas as pl
from jax.experimental.pallas import tpu as pltpu
from jax.sharding import PartitionSpec as P

R = 64
NS_STEPS = 8
CUTS = 16
COL = 8
SLICES = 12
SLOTS = 512
WIDTH = 1024
HALF = 256

F32 = jnp.float32
BF16 = jnp.bfloat16
HP = lax.Precision.HIGHEST
MESH = pl.DeviceIdType.MESH


def dot(a, b, ca=1, cb=0, precision=HP):
    return lax.dot_general(
        a, b, (((ca,), (cb,)), ((), ())), precision=precision, preferred_element_type=F32
    )


def fast(a, b, ca=1, cb=0):
    return dot(a, b, ca, cb, lax.Precision.DEFAULT)


def halves(x):
    high = x.astype(BF16)
    return high, (x - high.astype(F32)).astype(BF16)


def three(a, b_high, b_low, cb=0):
    a_high, a_low = halves(a)
    rows = a.shape[0]
    both = fast(jnp.concatenate([a_high, a_low], axis=0), b_high, 1, cb)
    return both[:rows] + both[rows:] + fast(a_high, b_low, 1, cb)


def iotas(shape):
    return lax.broadcasted_iota(jnp.int32, shape, 0), lax.broadcasted_iota(jnp.int32, shape, 1)


def pack(a):
    half = a.shape[0] // 2
    return jnp.concatenate([a[:half], a[half:]], axis=1)


def unpack(a):
    return jnp.concatenate([a[:, :R], a[:, R:]], axis=0)


def diagonals(a):
    rows, cols = iotas(a.shape)
    kept = jnp.where(rows == cols, a, 0.0)
    return jnp.sum(kept, axis=0, keepdims=True), jnp.sum(kept, axis=1, keepdims=True)


def inverse(gram):
    rows, cols = iotas(gram.shape)
    d_row, d_col = diagonals(gram)
    s_row, s_col = lax.rsqrt(d_row), lax.rsqrt(d_col)

    def sweep(t, a):
        at = [4 * t + i for i in range(4)]
        r = [jnp.sum(jnp.where(rows == p, a, 0.0), axis=0, keepdims=True) for p in at]
        c = [jnp.sum(jnp.where(cols == p, a, 0.0), axis=1, keepdims=True) for p in at]

        def pivot(m, n):
            return jnp.sum(jnp.where(rows[:, :1] == at[m], c[n], 0.0), axis=0, keepdims=True)

        a00, a01, a11 = pivot(0, 0), pivot(0, 1), pivot(1, 1)
        b00, b01, b10, b11 = pivot(0, 2), pivot(0, 3), pivot(1, 2), pivot(1, 3)
        k = 1.0 / (a00 * a11 - a01 * a01)
        i00, i01, i11 = a11 * k, -a01 * k, a00 * k
        t00, t01 = i00 * b00 + i01 * b10, i00 * b01 + i01 * b11
        t10, t11 = i01 * b00 + i11 * b10, i01 * b01 + i11 * b11
        s0 = pivot(2, 2) - (b00 * t00 + b10 * t10)
        s1 = pivot(2, 3) - (b00 * t01 + b10 * t11)
        s2 = pivot(3, 3) - (b01 * t01 + b11 * t11)
        m = 1.0 / (s0 * s2 - s1 * s1)
        r = [v + jnp.where(cols[:1] == p, 1.0, 0.0) for v, p in zip(r, at)]
        c = [v - jnp.where(rows[:, :1] == p, 1.0, 0.0) for v, p in zip(c, at)]
        y0, y1 = i00 * r[0] + i01 * r[1], i01 * r[0] + i11 * r[1]
        z0, z1 = r[2] - (b00 * y0 + b10 * y1), r[3] - (b01 * y0 + b11 * y1)
        u2, u3 = (s2 * m) * z0 - (s1 * m) * z1, (s0 * m) * z1 - (s1 * m) * z0
        u0, u1 = y0 - (t00 * u2 + t01 * u3), y1 - (t10 * u2 + t11 * u3)
        return a - ((c[0] * u0 + c[1] * u1) + (c[2] * u2 + c[3] * u3))

    return lax.fori_loop(0, R // 4, sweep, gram * s_col * s_row) * s_col * s_row


def kernel(
    len_ref, rec_ref, mask_ref, core_ref, column_ref, weight_ref,
    total_out, vt_out, core_out, gram_out,
    slab, vmask, keep, xsend, xrecv, zsend, zrecv, z0send, z0recv, x0send, x0recv, pall0, pall12,
    sgram, nall, yhi, ylo,
    sgbuf_y, sgbuf_q, cgbuf_z, cgbuf_x, hbuf_y, hbuf_z, hbuf_q, vsend, vrecv, vfull, fbuf, inv1, slice_gram, wide,
    slab_sem, xs, xr, zs, zr, z0s, z0r, x0s, x0r, ss, sr, gxs, gxr, gzs, gzr, g0s, g0r,
    ns, nr, ws, wr, cs, cr, hs, hr, vs, vr, as_, ar, fs, fr,
):
    c = lax.axis_index("cuts")
    l = lax.axis_index("col")
    z, x = l // 2, l % 2
    y, q = c // 4, c % 4
    other = z * 2 + (1 - x)

    sent = []

    def send(copy):
        copy.start()
        sent.append(copy)

    def col_to(src, dst, s, r, where):
        return pltpu.make_async_remote_copy(
            src_ref=src, dst_ref=dst, send_sem=s, recv_sem=r,
            device_id={"col": where}, device_id_type=MESH,
        )

    def cuts_to(src, dst, s, r, where):
        return pltpu.make_async_remote_copy(
            src_ref=src, dst_ref=dst, send_sem=s, recv_sem=r,
            device_id={"cuts": where}, device_id_type=MESH,
        )

    def col_at(d):
        return lax.rem(l + d, COL)

    def cuts_at(d):
        return lax.rem(c + d, CUTS)

    def z_plus(d):
        return lax.rem(z + d, 4)

    def exchange(buf, s, r, here, axis, stage):
        for d in (2, 1, 3):
            there = lax.rem(here + d, 4)
            if axis == "z":
                go, to = col_to, there * 2 + x
            else:
                go, to = cuts_to, (there * 4 + q if axis == "y" else y * 4 + there)
            if stage == "send":
                send(go(buf.at[here], buf.at[here], s.at[there], r.at[here], to))
            else:
                go(buf.at[there], buf.at[there], s.at[there], r.at[there], to).wait_recv()

    def sum4(buf):
        return (buf[0] + buf[1]) + (buf[2] + buf[3])

    def slab_copy(k):
        return pltpu.make_async_copy(rec_ref.at[k], slab.at[k], slab_sem.at[k])

    far = (2, 1, 3, 0)
    for d, j in ((2, 0), (2, 1), (2, 2), (1, 1), (1, 2), (1, 0), (3, 1), (3, 2), (3, 0), (0, 1), (0, 2), (0, 0)):
        slab_copy(z_plus(d) * 3 + j).start()

    barrier = pltpu.get_barrier_semaphore()
    pl.semaphore_signal(barrier, inc=1, device_id={"col": other}, device_id_type=MESH)
    for d in range(1, 4):
        for axis, to in (
            ("col", z_plus(d) * 2 + x),
            ("cuts", lax.rem(y + d, 4) * 4 + q),
            ("cuts", y * 4 + lax.rem(q + d, 4)),
        ):
            pl.semaphore_signal(barrier, inc=1, device_id={axis: to}, device_id_type=MESH)

    slot = lax.broadcasted_iota(jnp.int32, (1, SLOTS), 1)
    for k in range(SLICES):
        vmask[k:k + 1, :] = jnp.where((slot < len_ref[k]) & (mask_ref[k:k + 1, :] == 1), 1.0, 0.0)
    weight = weight_ref[...]
    column = column_ref[...]
    c_high, c_low = halves(column)
    c_both = jnp.concatenate([c_high, c_low], axis=0)
    cgbuf_z[z] = pack(dot(column, column, 1, 1))
    sgbuf_y[y] = pack(dot(weight, weight, 0, 0))

    def part_of(k, h):
        high, low = halves(slab[k, pl.ds(pl.multiple_of(h * HALF, HALF), HALF), :])
        both = fast(c_both, high, 1, 1)
        return both[:R] + both[R:] + fast(c_high, low, 1, 1)

    def pair(zz):
        def one(j, carry):
            k = zz * 3 + 1 + j
            slab_copy(k).wait()
            xsend[zz, j] = part_of(k, 1 - x)
            keep[zz, j] = part_of(k, x)
            return carry

        lax.fori_loop(0, 2, one, 0)

    def pair_send(zz):
        send(col_to(xsend.at[zz], xrecv.at[zz], xs.at[zz], xr.at[zz], other))

    def pair_sum(zz):
        col_to(xsend.at[zz], xrecv.at[zz], xs.at[zz], xr.at[zz], other).wait_recv()
        zsend[zz] = keep[zz] + xrecv[zz]

    def pair_pass(zz):
        pair_sum(zz)
        send(col_to(zsend.at[zz], zrecv.at[z], zs.at[zz], zr.at[z], zz * 2 + x))

    def single(zz):
        slab_copy(zz * 3).wait()

        def one(h, carry):
            z0send[zz, h] = part_of(zz * 3, h)
            return carry

        lax.fori_loop(0, 2, one, 0)

    def single_send(zz):
        send(col_to(z0send.at[zz], z0recv.at[z], z0s.at[zz], z0r.at[z], zz * 2 + x))

    single(z_plus(2))
    pl.semaphore_wait(barrier, 10)
    single_send(z_plus(2))
    pair(z_plus(2))
    pair_send(z_plus(2))
    exchange(sgbuf_y, ws.at[0], wr.at[0], y, "y", "send")
    exchange(cgbuf_z, cs, cr, z, "z", "send")
    pair(z_plus(1))
    pair_send(z_plus(1))
    single(z_plus(1))
    single_send(z_plus(1))
    pair_pass(z_plus(2))
    pair(z_plus(3))
    pair_send(z_plus(3))
    exchange(sgbuf_y, ws.at[0], wr.at[0], y, "y", "wait")
    sgbuf_q[q] = sum4(sgbuf_y)
    exchange(sgbuf_q, ws.at[1], wr.at[1], q, "q", "send")
    single(z_plus(3))
    single_send(z_plus(3))
    pair_pass(z_plus(1))
    exchange(cgbuf_z, cs, cr, z, "z", "wait")
    cgbuf_x[x] = sum4(cgbuf_z)
    send(col_to(cgbuf_x.at[x], cgbuf_x.at[x], cs.at[4], cr.at[4], other))
    pair(z)
    pair_send(z)
    single(z)
    pair_pass(z_plus(3))
    for d in far[:3]:
        zz = z_plus(d)
        col_to(z0send.at[zz], z0recv.at[zz], z0s.at[zz], z0r.at[zz], zz * 2 + x).wait_recv()
    x0send[...] = (z0send[z] + z0recv[z_plus(1)]) + (z0recv[z_plus(2)] + z0recv[z_plus(3)])
    send(col_to(x0send, x0recv, x0s, x0r, other))
    pair_sum(z)

    def mask_of(j, h):
        return vmask[pl.ds(z * 3 + j, 1), pl.ds(pl.multiple_of(h * HALF, HALF), HALF)]

    for d in far[:3]:
        zz = z_plus(d)
        col_to(zsend.at[zz], zrecv.at[zz], zs.at[zz], zr.at[zz], zz * 2 + x).wait_recv()
    partial_grams = []
    for j in range(2):
        total = (zsend[z, j] + zrecv[z_plus(1), j]) + (zrecv[z_plus(2), j] + zrecv[z_plus(3), j])
        total = total * mask_of(1 + j, x)
        pall12[z, x, j] = total
        partial_grams.append(dot(total, total, 1, 1))
    sgram[x] = jnp.concatenate(partial_grams, axis=1)
    send(col_to(sgram.at[x], sgram.at[x], ss, sr.at[x], other))
    for d in (1, 3, 2):
        zz = z_plus(d)
        send(col_to(pall12.at[z, x], pall12.at[z, x], gzs.at[zz], gzr.at[z], zz * 2 + x))
    send(col_to(pall12.at[z, x], pall12.at[z, x], gxs.at[z], gxr.at[z], other))

    exchange(sgbuf_q, ws.at[1], wr.at[1], q, "q", "wait")
    slice_gram[...] = unpack(sum4(sgbuf_q))
    col_to(cgbuf_x.at[1 - x], cgbuf_x.at[1 - x], cs.at[4], cr.at[4], other).wait_recv()
    inv1[...] = inverse(slice_gram[...] * unpack(cgbuf_x[0] + cgbuf_x[1]))
    k_of, s_of = iotas((SLICES, SLICES * R))
    spread = jnp.where(s_of // R == k_of, 1.0, 0.0)
    wide[...] = dot(weight, spread, 0, 0)
    col_to(x0send, x0recv, x0s, x0r, other).wait_recv()
    gram0 = jnp.zeros((R, R), F32)
    for h in range(2):
        total = (x0send[h] + x0recv[h]) * mask_of(0, h)
        pall0[z, h] = total
        gram0 = gram0 + dot(total, total, 1, 1)
    for d in far[:3]:
        zz = z_plus(d)
        send(col_to(pall0.at[z], pall0.at[z], g0s.at[zz], g0r.at[z], zz * 2 + x))
    col_to(sgram.at[1 - x], sgram.at[1 - x], ss, sr.at[1 - x], other).wait_recv()

    rows, cols = iotas((R, R))
    eye = jnp.where(rows == cols, 1.0, 0.0)
    both = sgram[0] + sgram[1]
    sums = [gram0, both[:, :R], both[:, R:]]
    grams, mixes, scales, wrows = [], [], [], []
    for j in range(3):
        wrow = weight_ref[pl.ds(z * 3 + j, 1), :]
        mix = core_ref[...] * wrow
        g = dot(dot(mix, sums[j]), mix, 1, 1)
        trace = jnp.sum(jnp.where(rows == cols, g, 0.0), axis=(0, 1), keepdims=True) + 1e-06
        grams.append(g / trace)
        mixes.append(mix)
        scales.append(lax.rsqrt(trace))
        wrows.append(wrow)

    left = lax.broadcasted_iota(jnp.int32, (1, 2 * R), 1) < R
    by0 = jnp.where(left, 2.25, 1.5)
    by1 = jnp.where(left, 1.5, 0.5)
    by2 = jnp.where(left, 0.25, 0.0)

    def newton(_, states):
        following = []
        for u in states:
            once = dot(u[:, :R], u)
            twice = dot(once[:, :R], u)
            following.append(by0 * u - by1 * once + by2 * twice)
        return following

    def forward(d):
        zz = z_plus(d)
        col_to(pall12.at[zz, x], pall12.at[zz, x], gzs.at[zz], gzr.at[zz], zz * 2 + x).wait_recv()
        send(col_to(pall12.at[zz, x], pall12.at[zz, x], gxs.at[zz], gxr.at[zz], other))

    state = [jnp.concatenate([g, eye], axis=1) for g in grams]
    state = lax.fori_loop(0, NS_STEPS - 1, newton, state)
    forward(1)
    forward(3)
    forward(2)
    h_sum = jnp.zeros((R, R), F32)
    turned_all = []
    for j in range(3):
        poly = (1.5 * state[j] - 0.5 * dot(state[j][:, :R], state[j]))[:, R:]
        turned = dot(mixes[j], poly, 0, 0) * scales[j]
        turned_all.append(turned)
        h_sum = h_sum + dot(turned, sums[j], 0, 0) * wrows[j]
    hbuf_y[y] = pack(h_sum)
    nall[z] = pack(jnp.concatenate(turned_all, axis=0))
    exchange(hbuf_y, hs.at[0], hr.at[0], y, "y", "send")
    exchange(nall, ns, nr, z, "z", "send")

    def second(k, proj):
        acc = jnp.zeros((R, WIDTH), F32)
        for h in range(2):
            high, low = halves(slab[k, h * HALF:(h + 1) * HALF, :])
            acc = acc + three(proj(h), high, low)
        high, low = halves(acc)
        at = pl.ds(pl.multiple_of(k * R, R), R)
        yhi[at, :] = high
        ylo[at, :] = low

    def second0(zz):
        second(zz * 3, lambda h: pall0[zz, h])

    def second12(zz):
        col_to(pall12.at[zz, 1 - x], pall12.at[zz, 1 - x], gxs.at[zz], gxr.at[zz], other).wait_recv()

        def one(j, carry):
            second(zz * 3 + 1 + j, lambda h: pall12[zz, h, j])
            return carry

        lax.fori_loop(0, 2, one, 0)

    exchange(pall0, g0s, g0r, z, "z", "wait")

    def all0(zz, carry):
        second0(zz)
        return carry

    lax.fori_loop(0, 4, all0, 0)
    second12(z)
    exchange(hbuf_y, hs.at[0], hr.at[0], y, "y", "wait")
    hbuf_z[z] = sum4(hbuf_y)
    exchange(hbuf_z, hs.at[1], hr.at[1], z, "z", "send")
    second12(z_plus(1))
    exchange(hbuf_z, hs.at[1], hr.at[1], z, "z", "wait")
    hbuf_q[q] = sum4(hbuf_z)
    exchange(hbuf_q, hs.at[2], hr.at[2], q, "q", "send")
    second12(z_plus(3))
    second12(z_plus(2))
    exchange(nall, ns, nr, z, "z", "wait")
    exchange(hbuf_q, hs.at[2], hr.at[2], q, "q", "wait")
    h_terms = unpack(sum4(hbuf_q))

    core_t = dot(inv1[...], h_terms, 1, 1)
    core_t = core_t * lax.rsqrt(jnp.sum(core_t * core_t, axis=1, keepdims=True) + 1e-06)
    core_gram = dot(core_t, core_t, 1, 1)
    stacked = jnp.concatenate([unpack(nall[i]) for i in range(4)], axis=0)
    mixed = dot(core_t, stacked, 1, 1)
    weighted = mixed * wide[...]
    v_local = three(weighted, yhi[...], ylo[...])
    for i in range(CUTS):
        part = v_local[(i // 8) * 32:(i // 8) * 32 + 32, (i % 8) * 128:(i % 8) * 128 + 128]
        vsend[i] = part
    vrecv[c] = vsend[c]
    for d in range(1, CUTS):
        to = cuts_at(d)
        send(cuts_to(vsend.at[to], vrecv.at[c], vs.at[to], vr.at[c], to))
    core_out[...] = dot(eye, core_t, 1, 1) * 8.0
    gram_out[...] = core_gram
    inv2 = inverse(slice_gram[...] * core_gram)
    for d in range(1, CUTS):
        frm = cuts_at(d)
        cuts_to(vsend.at[frm], vrecv.at[frm], vs.at[frm], vr.at[frm], frm).wait_recv()
    total = vrecv[0]
    for i in range(1, CUTS):
        total = total + vrecv[i]
    vfull[c] = total
    for d in range(1, CUTS):
        to = cuts_at(d)
        send(cuts_to(vfull.at[c], vfull.at[c], as_.at[to], ar.at[c], to))
    for d in range(1, CUTS):
        frm = cuts_at(d)
        cuts_to(vfull.at[frm], vfull.at[frm], as_.at[frm], ar.at[frm], frm).wait_recv()
    v_terms = jnp.concatenate(
        [jnp.concatenate([vfull[i * 8 + b] for b in range(8)], axis=1) for i in range(2)], axis=0
    )
    vt = dot(inv2, v_terms)
    v_gram = dot(vt, vt, 1, 1)
    found = mixed * three(vt, yhi[...], ylo[...], 1)
    w_terms = jnp.concatenate([dot(spread, found, 1, 1), jnp.zeros((4, R), F32)], axis=0)
    fbuf[l] = jnp.concatenate([pack(v_gram), pack(w_terms)], axis=0)
    for d in range(1, COL):
        to = col_at(d)
        send(col_to(fbuf.at[l], fbuf.at[l], fs.at[to], fr.at[l], to))
    vt_out[...] = vt
    for d in range(1, COL):
        frm = col_at(d)
        col_to(fbuf.at[frm], fbuf.at[frm], fs.at[frm], fr.at[frm], frm).wait_recv()
    total = fbuf[0]
    for i in range(1, COL):
        total = total + fbuf[i]
    total_out[...] = total

    for copy in sent:
        copy.wait_send()


def finish(total_ref, vt_ref, core_t_ref, gram_ref, core_out, column_out, weight_out):
    total = total_ref[...]
    v_gram = unpack(total[:32])
    w_terms = unpack(total[32:])[:SLICES]
    d_row, d_col = diagonals(v_gram)
    n_row, n_col = lax.rsqrt(d_row + 1e-06), lax.rsqrt(d_col + 1e-06)
    core_out[...] = core_t_ref[...]
    column_out[...] = vt_ref[...] * (n_col * (8192.0 ** 0.5))
    inv3 = inverse(gram_ref[...] * (v_gram * n_col * n_row))
    weight_out[...] = dot(w_terms * n_row, inv3)


def shards(records, row_lengths, row_mask, core_init, column_init, weight_init):
    vmem = pl.BlockSpec(memory_space=pltpu.VMEM)
    dma = pltpu.SemaphoreType.DMA
    four = dma((4,))
    chunk = pltpu.VMEM((4, 2, R, HALF), F32)
    square = jax.ShapeDtypeStruct((R, R), F32)
    found = pl.pallas_call(
        kernel,
        out_shape=(
            jax.ShapeDtypeStruct((40, 128), F32),
            jax.ShapeDtypeStruct((R, WIDTH), F32),
            square,
            square,
        ),
        in_specs=[pl.BlockSpec(memory_space=pltpu.SMEM), pl.BlockSpec(memory_space=pl.ANY)] + [vmem] * 4,
        out_specs=(vmem,) * 4,
        scratch_shapes=[
            pltpu.VMEM((SLICES, SLOTS, WIDTH), F32),
            pltpu.VMEM((SLICES, SLOTS), F32),
            chunk, chunk, chunk,
            chunk, chunk, chunk, chunk,
            pltpu.VMEM((2, R, HALF), F32),
            pltpu.VMEM((2, R, HALF), F32),
            chunk,
            pltpu.VMEM((4, 2, 2, R, HALF), F32),
            pltpu.VMEM((2, R, 128), F32),
            pltpu.VMEM((4, 3 * R // 2, 128), F32),
            pltpu.VMEM((SLICES * R, WIDTH), BF16),
            pltpu.VMEM((SLICES * R, WIDTH), BF16),
            pltpu.VMEM((4, 32, 128), F32),
            pltpu.VMEM((4, 32, 128), F32),
            pltpu.VMEM((4, 32, 128), F32),
            pltpu.VMEM((2, 32, 128), F32),
            pltpu.VMEM((4, 32, 128), F32),
            pltpu.VMEM((4, 32, 128), F32),
            pltpu.VMEM((4, 32, 128), F32),
            pltpu.VMEM((CUTS, 32, 128), F32),
            pltpu.VMEM((CUTS, 32, 128), F32),
            pltpu.VMEM((CUTS, 32, 128), F32),
            pltpu.VMEM((COL, 40, 128), F32),
            pltpu.VMEM((R, R), F32),
            pltpu.VMEM((R, R), F32),
            pltpu.VMEM((R, SLICES * R), F32),
            dma((SLICES,)),
            four, four, four, four, four, four,
            dma, dma,
            dma, dma((2,)),
            four, four, four, four, four, four,
            four, four,
            dma((2, 4)), dma((2, 4)),
            dma((5,)), dma((5,)),
            dma((3, 4)), dma((3, 4)),
            dma((CUTS,)), dma((CUTS,)),
            dma((CUTS,)), dma((CUTS,)),
            dma((COL,)), dma((COL,)),
        ],
        compiler_params=pltpu.CompilerParams(
            collective_id=0, has_side_effects=True, vmem_limit_bytes=60 * 1024 * 1024
        ),
    )(row_lengths, records, row_mask, core_init, column_init, weight_init)
    return pl.pallas_call(
        finish,
        out_shape=(
            square,
            jax.ShapeDtypeStruct((R, WIDTH), F32),
            jax.ShapeDtypeStruct((SLICES, R), F32),
        ),
        in_specs=[vmem] * 4,
        out_specs=(vmem,) * 3,
    )(*found)


def solution(mesh):
    in_specs = (
        P("cuts", None, "col"),
        P("cuts"),
        P("cuts", None),
        P(),
        P(None, "col"),
        P("cuts", None),
    )
    out_specs = (P(), P(None, "col"), P("cuts", None))
    return jax.shard_map(shards, mesh=mesh, in_specs=in_specs, out_specs=out_specs, check_vma=False)
```
